256 devices in a mesh: member: 4 (over x), tile: 64 (over z, y, core).
Axes of the slice: x: 4, y: 4, z: 8, core: 2. Of those that a mesh axis runs over, the one named last changes fastest.
Arguments:
- member_state: float32 [40, 16, 1536, 128], P('member', None, 'tile'), may hold values from -6 to 6
- courant: float32 [2, 16, 1536, 128], P(None, None, 'tile'), may hold values from -0.45 to 0.45
- obs_col: int32 [131072], P(('member', 'tile')), may hold values from 0 to 767
- obs_lev: int32 [131072], P(('member', 'tile')), may hold values from 0 to 15
- innovation: float32 [131072], P(('member', 'tile')), may hold values from -24 to 24
- obs_var: float32 [131072], P(('member', 'tile')), may hold values from 0.5 to 4
- mode_waves: int32 [12], replicated, may hold values from 0 to 15
Outputs:
- advanced: float32 [40, 16, 1536, 128], P('member', None, 'tile')
- increment: float32 [16, 196608], P(None, ('member', 'tile'))
The draws below stay inside these ranges and needn't reach their ends.
All inputs are finite; a program needn't handle non-finite values.
Results may differ from the reference program's by a relative error of at most 0.0003.
Values sent between devices are 32-bit elements; how exact they have to be, the bound alone decides.
A program may use at most 128 MiB of HBM per device.

```python
import math
import jax
import jax.numpy as jnp
from jax import lax

MEMBERS = 40
MODES = 12
LEV = 16
CY = 128
NOBS = 512
NX = 1536
OWN = 768
COLS_ALL = 196608
OBS_ALL = 131072
N_MEMBER = 4
N_TILE = 64


def with_ends(entries, key, least, high):
    dims = entries.shape
    place = [jax.random.randint(jax.random.fold_in(key, axis), (), 0, dims[axis]) for axis in range(len(dims))]
    entries = entries.at[tuple(place)].set(least)
    longest = dims.index(max(dims))
    place[longest] = (place[longest] + 1) % dims[longest]
    return entries.at[tuple(place)].set(high)


def steps_of(rng, shape, pieces, smallest, largest):
    loudness, own = 1.0, jax.random.fold_in(rng, 6)
    for axis_at, parts in pieces:
        steps = jnp.exp(jax.random.uniform(jax.random.fold_in(own, axis_at), (parts,), jnp.float32, smallest / len(pieces), largest / len(pieces)))
        loudness = loudness * jnp.repeat(steps, shape[axis_at] // parts).reshape([-1 if axis == axis_at else 1 for axis in range(len(shape))])
    return loudness


def normal_values(own_key, shape, spread, most, cuts=(), kind=jnp.bfloat16):
    array = spread * jax.random.normal(own_key, shape, jnp.float32)
    if cuts:
        array = array * steps_of(own_key, shape, cuts, -0.22, 0.18)
    return jnp.clip(array, -most, most).astype(kind)


def setup_inputs(seed: int = 0) -> dict:
    key_list = jax.random.split(jax.random.key(seed), 8)
    return {
        "member_state": normal_values(key_list[0], (MEMBERS, LEV, NX, CY), 1.0, 6.0, ((0, 4), (2, 64)), jnp.float32),
        "courant": jnp.clip(jax.random.uniform(key_list[1], (2, LEV, NX, CY), jnp.float32, -0.45, 0.45) * steps_of(key_list[1], (2, LEV, NX, CY), ((2, 64),), -0.4, 0.0), -0.45, 0.45),
        "obs_col": with_ends(jax.random.randint(key_list[2], (OBS_ALL,), 0, OWN), jax.random.fold_in(key_list[2], 1), 0, OWN - 1).astype(jnp.int32),
        "obs_lev": with_ends(jax.random.randint(key_list[3], (OBS_ALL,), 0, LEV), jax.random.fold_in(key_list[3], 1), 0, LEV - 1).astype(jnp.int32),
        "innovation": normal_values(key_list[4], (OBS_ALL,), 4.0, 24.0, ((0, 256),), jnp.float32),
        "obs_var": jnp.clip(jnp.exp(math.log(4.0) - 2.0794415 * jax.random.uniform(key_list[5], (OBS_ALL,), jnp.float32) ** steps_of(key_list[5], (OBS_ALL,), ((0, 256),), -0.2, 0.2)), 0.5, 4.0),
        "mode_waves": with_ends(jax.random.randint(key_list[6], (MODES,), 0, LEV), jax.random.fold_in(key_list[6], 1), 0, LEV - 1).astype(jnp.int32),
    }


def wrap_pad(field):
    return jnp.concatenate([field[:, :, -1:], field, field[:, :, :1]], axis=2)

def upwind(padded, courant):
    centre = padded[:, :, 1:-1]
    west = padded[:, :, :-2]
    east = padded[:, :, 2:]
    south = jnp.roll(centre, 1, axis=3)
    north = jnp.roll(centre, -1, axis=3)
    along_x = courant[0]
    along_y = courant[1]
    return centre - jnp.maximum(along_x, 0.0) * (centre - west) - jnp.minimum(along_x, 0.0) * (east - centre) - jnp.maximum(along_y, 0.0) * (centre - south) - jnp.minimum(along_y, 0.0) * (north - centre)

def mode_profiles(mode_waves):
    heights = jnp.arange(LEV).astype(jnp.float32)
    waves = mode_waves.astype(jnp.float32)
    scales = 1.0 / jnp.sqrt(1.0 + jnp.arange(MODES).astype(jnp.float32))
    return scales[:, None] * jnp.cos(jnp.pi * waves[:, None] * (heights[None, :] + 0.5) / LEV)

def reference(member_state, courant, obs_col, obs_lev, innovation, obs_var, mode_waves):
    highest = lax.Precision.HIGHEST
    field = member_state
    for passes in range(2):
        field = upwind(wrap_pad(field), courant)
    advanced = field
    total = MEMBERS
    owned = advanced.reshape(total, LEV, N_TILE, N_MEMBER, OWN).transpose(0, 1, 3, 2, 4).reshape(total, LEV, COLS_ALL)
    anomaly = (owned - lax.optimization_barrier(jnp.mean(owned, axis=0, keepdims=True))) / jnp.sqrt(jnp.float32(total - 1))
    blocks = (jnp.arange(OBS_ALL) // NOBS).astype(jnp.int32)
    flat_index = obs_lev.astype(jnp.int32) * COLS_ALL + blocks * OWN + obs_col.astype(jnp.int32)
    picked = jnp.take(anomaly.reshape(total, LEV * COLS_ALL), flat_index, axis=1)
    weighted = picked / obs_var[None, :]
    profiles = mode_profiles(mode_waves)

    def level_terms(level):
        masked = weighted * (obs_lev == level).astype(jnp.float32)[None, :]
        return (jnp.dot(masked, picked.T, precision=highest), jnp.dot(masked, innovation, precision=highest))
    sums, cross = lax.map(level_terms, jnp.arange(LEV).astype(jnp.int32))
    width = total * MODES
    gram = jnp.einsum('lkm,jl,il->kjmi', sums, profiles, profiles, precision=highest).reshape(width, width)
    rhs = jnp.einsum('lk,jl->kj', cross, profiles, precision=highest).reshape(width)
    system = jnp.eye(width, dtype=jnp.float32) + gram
    factor = jnp.linalg.cholesky(system)
    weights = jax.scipy.linalg.cho_solve((factor, True), rhs)
    coeffs = jnp.einsum('kj,jl->kl', weights.reshape(total, MODES), profiles, precision=highest)
    increment = jnp.einsum('klc,kl->lc', anomaly, coeffs, precision=highest)
    return (advanced, increment)
```

```python
import functools
import math

import jax
import jax.numpy as jnp
from jax import lax
from jax.experimental import pallas as pl
from jax.experimental.pallas import tpu as pltpu
from jax.sharding import PartitionSpec as P

MESH = pl.DeviceIdType.MESH
HIGHEST = lax.Precision.HIGHEST
ANY = pl.BlockSpec(memory_space=pl.ANY)
VMEM = pl.BlockSpec(memory_space=pltpu.VMEM)
SMEM = pl.BlockSpec(memory_space=pltpu.SMEM)
N_Y = 4
N_CORE = 2
GROUP = 4
LOCAL = 10
MEMBERS = 40
MODES = 12
LEV = 16
X = 24
CY = 128
RUN = 6
ROWS = LOCAL * LEV
NOBS = 512
TILES = 30
BLOCK = 120
WIDE = 768
VMEM_LIMIT = 48 * 1024 * 1024


def remote(src, dst, send, recv, member, tile):
    return pltpu.make_async_remote_copy(
        src_ref=src,
        dst_ref=dst,
        send_sem=send,
        recv_sem=recv,
        device_id={"member": member, "tile": tile},
        device_id_type=MESH,
    )


def upwind(centre, west, east, cx, cy):
    cx = cx[None]
    cy = cy[None]
    south = pltpu.roll(centre, 1, 2)
    north = pltpu.roll(centre, CY - 1, 2)
    from_x = jnp.where(cx > 0.0, west, east)
    from_y = jnp.where(cy > 0.0, south, north)
    return centre - jnp.abs(cx) * (centre - from_x) - jnp.abs(cy) * (centre - from_y)


def front(
    g1,
    g2,
    piece,
    state_ref,
    courant_ref,
    col_ref,
    lev_ref,
    innov_ref,
    var_ref,
    field_out,
    rows_out,
    sums_ref,
    state,
    courant,
    q0,
    q1,
    q2,
    wind,
    field,
    obs,
    pick,
    held,
    weighted,
    part,
    got,
    red,
    load_sem,
    halo_send,
    halo_recv,
    obs_send,
    obs_recv,
    pick_send,
    pick_recv,
    rs_send,
    rs_recv,
    ex_send,
    ex_recv,
    ag_send,
    ag_recv,
    out_sem,
):
    tiles = lax.axis_size("tile")
    me = lax.axis_index("member")
    tile = lax.axis_index("tile")
    core = lax.rem(tile, N_CORE)
    y = lax.rem(tile // N_CORE, N_Y)
    z = tile // (N_CORE * N_Y)
    right = lax.rem(tile + 1, tiles)
    left = lax.rem(tile + tiles - 1, tiles)
    a = me * N_Y + y
    b = z * N_CORE + core

    def peer_a(r):
        other = lax.rem(a + r, g1)
        return other, other // N_Y, (z * N_Y + lax.rem(other, N_Y)) * N_CORE + core

    def peer_b(r):
        other = lax.rem(b + r, g2)
        return other, me, ((other // N_CORE) * N_Y + y) * N_CORE + lax.rem(other, N_CORE)

    loads = [
        pltpu.make_async_copy(state_ref, state, load_sem.at[0]),
        pltpu.make_async_copy(courant_ref, courant, load_sem.at[1]),
    ]
    for copy in loads:
        copy.start()

    barrier = pltpu.get_barrier_semaphore()
    for other in (left, right):
        pl.semaphore_signal(barrier, 1, device_id={"member": me, "tile": other}, device_id_type=MESH)

    def greet_a(r, _):
        _, m, t = peer_a(r)
        pl.semaphore_signal(barrier, 1, device_id={"member": m, "tile": t}, device_id_type=MESH)
        return 0

    def greet_b(r, _):
        _, m, t = peer_b(r)
        pl.semaphore_signal(barrier, 1, device_id={"member": m, "tile": t}, device_id_type=MESH)
        return 0

    lax.fori_loop(1, g1, greet_a, 0)
    lax.fori_loop(1, g2, greet_b, 0)

    obs[me] = jnp.broadcast_to(lev_ref[...] * 1024 + col_ref[...], (8, NOBS))
    for copy in loads:
        copy.wait()

    def turn(x, _):
        q0[x + 2] = state[pl.ds(x, ROWS, stride=X), :]
        wind[x + 1] = courant[pl.ds(x, 2 * LEV, stride=X), :]
        return 0

    for x in (0, 1, 22, 23):
        turn(x, 0)

    pl.semaphore_wait(barrier, 2 + (g1 - 1) + (g2 - 1))

    halos = [
        remote(q0.at[pl.ds(X, 2)], q0.at[pl.ds(0, 2)], halo_send.at[0], halo_recv.at[0], me, right),
        remote(wind.at[X], wind.at[0], halo_send.at[1], halo_recv.at[1], me, right),
        remote(q0.at[pl.ds(2, 2)], q0.at[pl.ds(X + 2, 2)], halo_send.at[2], halo_recv.at[2], me, left),
        remote(wind.at[1], wind.at[X + 1], halo_send.at[3], halo_recv.at[3], me, left),
    ]
    for copy in halos:
        copy.start()
    obs_copies = []
    for r in range(1, GROUP):
        to = lax.rem(me + r, GROUP)
        copy = remote(obs.at[me], obs.at[me], obs_send.at[r - 1], obs_recv.at[r - 1], to, tile)
        copy.start()
        obs_copies.append(copy)

    lax.fori_loop(2, 22, turn, 0)

    def first(i, _):
        w = wind[i]
        new = upwind(
            q0[i + 1].reshape(LOCAL, LEV, CY),
            q0[i].reshape(LOCAL, LEV, CY),
            q0[i + 2].reshape(LOCAL, LEV, CY),
            w[:LEV],
            w[LEV:],
        )
        q1[i] = new.reshape(ROWS, CY)
        return 0

    def second(i, _):
        w = wind[i + 1]
        new = upwind(
            q1[i + 1].reshape(LOCAL, LEV, CY),
            q1[i].reshape(LOCAL, LEV, CY),
            q1[i + 2].reshape(LOCAL, LEV, CY),
            w[:LEV],
            w[LEV:],
        ).reshape(ROWS, CY)
        q2[i] = new
        field[pl.ds(i, ROWS, stride=X), :] = new
        return 0

    lax.fori_loop(2, X, first, 0)
    for copy in halos:
        copy.wait_recv()
    for i in (0, 1, X, X + 1):
        first(i, 0)
    lax.fori_loop(0, X, second, 0)

    outs = [
        pltpu.make_async_copy(field, field_out, out_sem.at[0]),
        pltpu.make_async_copy(q2, rows_out, out_sem.at[1]),
    ]
    for copy in outs:
        copy.start()

    for copy in obs_copies:
        copy.wait_recv()

    sub_y = lax.broadcasted_iota(jnp.int32, (CY, NOBS), 0)
    sub_l = lax.broadcasted_iota(jnp.int32, (LEV, NOBS), 0)

    def pick_for(owner):
        code = obs[owner][:1]
        spot = code & 1023
        row = lax.shift_right_logical(code, 10) * 8 + lax.shift_right_logical(spot, 7)
        hot = (sub_y == (spot & 127)).astype(jnp.bfloat16)
        total = jnp.zeros((LOCAL, LEV, NOBS), jnp.float32)
        for x in range(RUN):
            cells = q2[owner * RUN + x]
            high = cells.astype(jnp.bfloat16)
            rest = cells - high.astype(jnp.float32)
            mid = rest.astype(jnp.bfloat16)
            low = (rest - mid.astype(jnp.float32)).astype(jnp.bfloat16)
            found = sum(jnp.dot(p, hot, preferred_element_type=jnp.float32) for p in (high, mid, low))
            here = (row == sub_l * 8 + x)[None]
            total = total + jnp.where(here, found.reshape(LOCAL, LEV, NOBS), 0.0)
        return jnp.sum(total, axis=1)

    pick_copies = []
    for r in range(1, GROUP):
        to = lax.rem(me + r, GROUP)
        pick[r - 1, :LOCAL] = pick_for(to)
        pick[r - 1, LOCAL:] = jnp.zeros((16 - LOCAL, NOBS), jnp.float32)
        copy = remote(pick.at[r - 1], held.at[me], pick_send.at[r - 1], pick_recv.at[r - 1], to, tile)
        copy.start()
        pick_copies.append(copy)
    held[me, :LOCAL] = pick_for(me)
    for copy in pick_copies:
        copy.wait_recv()

    picked = jnp.concatenate([held[m][:LOCAL] for m in range(GROUP)], axis=0)
    mean = jnp.sum(picked, axis=0, keepdims=True) * (1.0 / MEMBERS)
    anomaly = (picked - mean) * (1.0 / math.sqrt(MEMBERS - 1.0))
    inverse = 1.0 / var_ref[...]
    scaled = anomaly * inverse
    innov = innov_ref[...] * inverse
    level = lev_ref[...]
    for l in range(LEV):
        weighted[l * MEMBERS : (l + 1) * MEMBERS] = jnp.where(level == l, scaled, 0.0)
    own_level = lax.broadcasted_iota(jnp.int32, (LEV, NOBS), 0) == level
    weighted[LEV * MEMBERS : LEV * MEMBERS + LEV] = jnp.where(own_level, innov, 0.0)
    weighted[LEV * MEMBERS + LEV :] = jnp.zeros((WIDE - LEV * MEMBERS - LEV, NOBS), jnp.float32)
    sums = lax.dot_general(
        anomaly,
        weighted[...],
        (((1,), (1,)), ((), ())),
        precision=HIGHEST,
        preferred_element_type=jnp.float32,
    )
    for q in range(TILES):
        s, c = q // 6, q % 6
        part[q // piece, (q % piece) * 8 : (q % piece) * 8 + 8] = sums[s * 8 : s * 8 + 8, c * 128 : c * 128 + 128]
    for q in range(TILES, g1 * piece):
        part[q // piece, (q % piece) * 8 : (q % piece) * 8 + 8] = jnp.zeros((8, 128), jnp.float32)

    def rs_copy(r):
        other, m, t = peer_a(r)
        return remote(part.at[other], got.at[r - 1], rs_send.at[r - 1], rs_recv.at[r - 1], m, t)

    def ex_copy(r):
        other, m, t = peer_b(r)
        return remote(red.at[b], red.at[b], ex_send.at[r - 1], ex_recv.at[r - 1], m, t)

    def ag_copy(r):
        other, m, t = peer_a(r)
        return remote(sums_ref.at[a], sums_ref.at[a], ag_send.at[r - 1], ag_recv.at[r - 1], m, t)

    for r in range(1, g1):
        rs_copy(r).start()
    for r in range(1, g1):
        rs_copy(r).wait_recv()
    red[b] = part[a] + jnp.sum(got[...], axis=0)
    for r in range(1, g2):
        ex_copy(r).start()
    for r in range(1, g2):
        ex_copy(r).wait_recv()
    sums_ref[a] = jnp.sum(red[...], axis=0)
    for r in range(1, g1):
        ag_copy(r).start()
    for r in range(1, g1):
        ag_copy(r).wait_recv()

    for copy in halos + obs_copies + pick_copies:
        copy.wait_send()
    for r in range(1, g1):
        rs_copy(r).wait_send()
        ag_copy(r).wait_send()
    for r in range(1, g2):
        ex_copy(r).wait_send()
    for copy in outs:
        copy.wait()


def inverse_of(tiles):
    lane = lax.broadcasted_iota(jnp.int32, (8, 128), 1)
    sub = lax.broadcasted_iota(jnp.int32, (8, 128), 0)
    count = len(tiles)
    tiles = list(tiles)
    for p in range(count):
        rows = tiles[p]
        for j in range(8):
            c = 8 * p + j
            column = jnp.broadcast_to(rows[:, c : c + 1], (8, 128))
            pivot = jnp.broadcast_to(column[j : j + 1], (8, 128))
            line = jnp.broadcast_to(rows[j : j + 1], (8, 128))
            line = jnp.where(lane == c, 1.0, line) / pivot
            base = jnp.where((lane == c) | (sub == j), 0.0, rows)
            rows = base - jnp.where(sub == j, -1.0, column) * line
        tiles[p] = rows
        inside = (lane >= 8 * p) & (lane < 8 * p + 8)
        lines = [jnp.broadcast_to(rows[j : j + 1], (8, 128)) for j in range(8)]
        for t in range(count):
            if t == p:
                continue
            old = tiles[t]
            new = jnp.where(inside, 0.0, old)
            for j in range(8):
                c = 8 * p + j
                new = new - jnp.broadcast_to(old[:, c : c + 1], (8, 128)) * lines[j]
            tiles[t] = new
    return tiles


def dot(left, right):
    return jnp.dot(left, right, precision=HIGHEST, preferred_element_type=jnp.float32)


def solve(piece, sums_ref, waves_ref, field_ref, coeff_ref, advanced_ref, gram, left, right, system, block, line, copy_sem):
    keep = pltpu.make_async_copy(field_ref, advanced_ref, copy_sem)
    keep.start()
    for q in range(TILES):
        s, c = q // 6, q % 6
        gram[s * 8 : s * 8 + 8, c * 128 : c * 128 + 128] = sums_ref[q // piece, (q % piece) * 8 : (q % piece) * 8 + 8]

    def cosines(wave, level):
        return jnp.cos(jnp.pi * wave * (level.astype(jnp.float32) + 0.5) / LEV)

    def by_mode(mode):
        wave = jnp.zeros(mode.shape, jnp.float32)
        scale = jnp.zeros(mode.shape, jnp.float32)
        for j in range(MODES):
            wave = jnp.where(mode == j, waves_ref[j].astype(jnp.float32), wave)
            scale = jnp.where(mode == j, 1.0 / math.sqrt(1.0 + j), scale)
        return wave, scale

    def iota(shape, axis):
        return lax.broadcasted_iota(jnp.int32, shape, axis)

    lane = iota((16, WIDE), 1)
    level = jnp.where(lane < LEV * MEMBERS, lane // MEMBERS, lane - LEV * MEMBERS)
    wave, scale = by_mode(iota((16, WIDE), 0))
    line[...] = jnp.where(lane < LEV * MEMBERS + LEV, scale * cosines(wave, level), 0.0)
    for i in range(MODES):
        left[i * MEMBERS : (i + 1) * MEMBERS] = gram[...] * line[i : i + 1]
    lane = iota((16, 512), 1)
    inner = lane % 128
    mode = jnp.where(inner < BLOCK, (lane // 128) * 3 + inner // MEMBERS, MODES)
    wave, scale = by_mode(mode)
    table = scale * cosines(wave, iota((16, 512), 0))
    lane = iota((MEMBERS, 512), 1)
    same = ((lane % 128) % MEMBERS) == iota((MEMBERS, 512), 0)
    for l in range(LEV):
        right[l * MEMBERS : (l + 1) * MEMBERS] = jnp.where(same, table[l : l + 1], 0.0)
    spot = 3 * 128 + BLOCK
    tail = WIDE - LEV * MEMBERS
    at = (iota((tail, 512), 1) == spot) & (iota((tail, 512), 0) < LEV)
    right[LEV * MEMBERS :] = jnp.where(at, 1.0, 0.0)
    system[...] = dot(left[...], right[...])

    diag = (iota((BLOCK, 128), 0) == iota((BLOCK, 128), 1)).astype(jnp.float32)
    for p in range(4):
        here = slice(p * BLOCK, (p + 1) * BLOCK)
        cols = slice(p * 128, (p + 1) * 128)
        own = system[here, cols] + diag
        own = jnp.where(iota((BLOCK, 128), 1) < BLOCK, own, 0.0)
        done = inverse_of([own[8 * t : 8 * t + 8] for t in range(BLOCK // 8)])
        for t in range(BLOCK // 8):
            block[8 * t : 8 * t + 8] = done[t]
        rest = slice(min((p + 1) * 128, 384), 512)
        new = dot(block[...][:, :BLOCK], system[here, rest])
        for q in range(4):
            if q != p:
                there = slice(q * BLOCK, (q + 1) * BLOCK)
                system[there, rest] = system[there, rest] - dot(system[there, cols][:, :BLOCK], new)
        system[here, rest] = new

    lane = iota((16, 128), 1)
    wave, scale = by_mode(iota((16, 128), 0))
    table = jnp.where(lane < LEV, scale * cosines(wave, lane), 0.0)
    total = jnp.zeros((MEMBERS, 128), jnp.float32)
    for j in range(MODES):
        weight = system[j * MEMBERS : (j + 1) * MEMBERS, 384:512][:, BLOCK : BLOCK + 1]
        total = total + weight * table[j : j + 1]
    mean = jnp.sum(total, axis=0, keepdims=True) * (1.0 / MEMBERS)
    total = (total - mean) * (1.0 / math.sqrt(MEMBERS - 1.0))
    turned = jnp.concatenate([total, jnp.zeros((128 - MEMBERS, 128), jnp.float32)], axis=0).T[:LEV]
    for k in range(MEMBERS):
        coeff_ref[k] = jnp.broadcast_to(turned[:, k : k + 1], (LEV, 128))
    keep.wait()


def finish(coeff_ref, rows_ref, out_ref, part, got, send_sem, recv_sem):
    me = lax.axis_index("member")
    tile = lax.axis_index("tile")
    barrier = pltpu.get_barrier_semaphore()
    for r in range(1, GROUP):
        to = lax.rem(me + r, GROUP)
        pl.semaphore_signal(barrier, 1, device_id={"member": to, "tile": tile}, device_id_type=MESH)

    def run_for(owner, slot):
        for x in range(RUN):
            total = jnp.zeros((LEV, CY), jnp.float32)
            for k in range(LOCAL):
                total = total + rows_ref[owner * RUN + x, k * LEV : (k + 1) * LEV] * coeff_ref[me * LOCAL + k]
            part[slot, x] = total

    copies = []
    for r in range(1, GROUP):
        to = lax.rem(me + r, GROUP)
        run_for(to, r)
        if r == 1:
            pl.semaphore_wait(barrier, GROUP - 1)
        copy = remote(part.at[r], got.at[r - 1], send_sem.at[r - 1], recv_sem.at[r - 1], to, tile)
        copy.start()
        copies.append(copy)
    run_for(me, 0)
    for copy in copies:
        copy.wait_recv()
    for x in range(RUN):
        out_ref[:, x * CY : (x + 1) * CY] = part[0, x] + got[0, x] + got[1, x] + got[2, x]
    for copy in copies:
        copy.wait_send()


def on_device(member_state, courant, obs_col, obs_lev, innovation, obs_var, mode_waves):
    tiles = lax.axis_size("tile")
    g1 = GROUP * N_Y
    g2 = tiles // N_Y
    piece = -(-TILES // g1)
    f32 = jnp.float32
    dma = pltpu.SemaphoreType.DMA
    shape = member_state.shape
    field, rows, sums = pl.pallas_call(
        functools.partial(front, g1, g2, piece),
        out_shape=[
            jax.ShapeDtypeStruct((ROWS * X, CY), f32),
            jax.ShapeDtypeStruct((X, ROWS, CY), f32),
            jax.ShapeDtypeStruct((g1, piece * 8, 128), f32),
        ],
        in_specs=[ANY, ANY, VMEM, VMEM, VMEM, VMEM],
        out_specs=[ANY, ANY, VMEM],
        scratch_shapes=[
            pltpu.VMEM((ROWS * X, CY), f32),
            pltpu.VMEM((2 * LEV * X, CY), f32),
            pltpu.VMEM((X + 4, ROWS, CY), f32),
            pltpu.VMEM((X + 2, ROWS, CY), f32),
            pltpu.VMEM((X, ROWS, CY), f32),
            pltpu.VMEM((X + 2, 2 * LEV, CY), f32),
            pltpu.VMEM((ROWS * X, CY), f32),
            pltpu.VMEM((GROUP, 8, NOBS), jnp.int32),
            pltpu.VMEM((GROUP - 1, 16, NOBS), f32),
            pltpu.VMEM((GROUP, 16, NOBS), f32),
            pltpu.VMEM((WIDE, NOBS), f32),
            pltpu.VMEM((g1, piece * 8, 128), f32),
            pltpu.VMEM((g1 - 1, piece * 8, 128), f32),
            pltpu.VMEM((g2, piece * 8, 128), f32),
            dma((2,)),
            dma((4,)),
            dma((4,)),
            dma((GROUP - 1,)),
            dma((GROUP - 1,)),
            dma((GROUP - 1,)),
            dma((GROUP - 1,)),
            dma((g1 - 1,)),
            dma((g1 - 1,)),
            dma((g2 - 1,)),
            dma((g2 - 1,)),
            dma((g1 - 1,)),
            dma((g1 - 1,)),
            dma((2,)),
        ],
        compiler_params=pltpu.CompilerParams(
            collective_id=0, has_side_effects=True, vmem_limit_bytes=VMEM_LIMIT
        ),
        name="front",
    )(
        member_state.reshape(ROWS * X, CY),
        courant.reshape(2 * LEV * X, CY),
        obs_col.reshape(1, NOBS),
        obs_lev.reshape(1, NOBS),
        innovation.reshape(1, NOBS),
        obs_var.reshape(1, NOBS),
    )
    coeffs, advanced = pl.pallas_call(
        functools.partial(solve, piece),
        out_shape=[
            jax.ShapeDtypeStruct((MEMBERS, LEV, 128), f32),
            jax.ShapeDtypeStruct((ROWS * X, CY), f32),
        ],
        in_specs=[VMEM, SMEM, ANY],
        out_specs=[VMEM, ANY],
        scratch_shapes=[
            pltpu.VMEM((MEMBERS, WIDE), f32),
            pltpu.VMEM((MODES * MEMBERS, WIDE), f32),
            pltpu.VMEM((WIDE, 512), f32),
            pltpu.VMEM((MODES * MEMBERS, 512), f32),
            pltpu.VMEM((BLOCK, 128), f32),
            pltpu.VMEM((16, WIDE), f32),
            dma,
        ],
        compiler_params=pltpu.CompilerParams(vmem_limit_bytes=VMEM_LIMIT),
        name="solve",
    )(sums, mode_waves, field)
    increment = pl.pallas_call(
        finish,
        out_shape=jax.ShapeDtypeStruct((LEV, RUN * CY), f32),
        in_specs=[VMEM, VMEM],
        out_specs=VMEM,
        scratch_shapes=[
            pltpu.VMEM((GROUP, RUN, LEV, CY), f32),
            pltpu.VMEM((GROUP - 1, RUN, LEV, CY), f32),
            dma((GROUP - 1,)),
            dma((GROUP - 1,)),
        ],
        compiler_params=pltpu.CompilerParams(
            collective_id=1, has_side_effects=True, vmem_limit_bytes=VMEM_LIMIT
        ),
        name="finish",
    )(coeffs, rows)
    return advanced.reshape(shape), increment


def solution(mesh):
    in_specs = (
        P("member", None, "tile", None),
        P(None, None, "tile", None),
        P(("member", "tile")),
        P(("member", "tile")),
        P(("member", "tile")),
        P(("member", "tile")),
        P(),
    )
    out_specs = (P("member", None, "tile", None), P(None, ("member", "tile")))
    return jax.shard_map(
        on_device, mesh=mesh, in_specs=in_specs, out_specs=out_specs, check_vma=False
    )
```

```python
import functools
import math

import jax
import jax.numpy as jnp
from jax import lax
from jax.experimental import pallas as pl
from jax.experimental.pallas import tpu as pltpu
from jax.sharding import PartitionSpec as P

MESH = pl.DeviceIdType.MESH
HIGHEST = lax.Precision.HIGHEST
ANY = pl.BlockSpec(memory_space=pl.ANY)
VMEM = pl.BlockSpec(memory_space=pltpu.VMEM)
SMEM = pl.BlockSpec(memory_space=pltpu.SMEM)
N_Y = 4
N_CORE = 2
GROUP = 4
LOCAL = 10
MEMBERS = 40
MODES = 12
LEV = 16
X = 24
CY = 128
RUN = 6
ROWS = LOCAL * LEV
NOBS = 512
TILES = 30
BLOCK = 120
WIDE = 768
VMEM_LIMIT = 56 * 1024 * 1024


def remote(src, dst, send, recv, member, tile):
    return pltpu.make_async_remote_copy(
        src_ref=src,
        dst_ref=dst,
        send_sem=send,
        recv_sem=recv,
        device_id={"member": member, "tile": tile},
        device_id_type=MESH,
    )


def upwind(centre, west, east, wind):
    cx = wind[:LEV][None]
    cy = wind[LEV:][None]
    lane = lax.broadcasted_iota(jnp.int32, (1, LEV, CY), 2)
    source = jnp.broadcast_to((lane + jnp.where(cy > 0.0, -1, 1)) & (CY - 1), (LOCAL, LEV, CY))
    from_y = jnp.take_along_axis(centre, source.reshape(ROWS, CY), axis=1)
    centre, west, east, from_y = (v.reshape(LOCAL, LEV, CY) for v in (centre, west, east, from_y))
    from_x = jnp.where(cx > 0.0, west, east)
    new = centre - jnp.abs(cx) * (centre - from_x) - jnp.abs(cy) * (centre - from_y)
    return new.reshape(ROWS, CY)


def offset(group, r):
    member = shift = 0
    for bits, place in reversed(group):
        part = r & ((1 << bits) - 1)
        r >>= bits
        if place is None:
            member = part
        else:
            shift |= part << place
    return member, shift


def far_first(group):
    def hops(r):
        total = 0.0
        for bits, place in reversed(group):
            part = r & ((1 << bits) - 1)
            r >>= bits
            if place != 0:
                total += (0.0, 1.0, 2.0, 1.0)[part] if bits == 2 else (0.0, 1.0, 2.0, 2.2, 4.0, 3.0, 2.4, 1.5)[part]
        return total

    count = 1 << sum(bits for bits, _ in group)
    return sorted(range(1, count), key=lambda r: -hops(r))


def front(
    plane,
    depth,
    piece,
    state_ref,
    courant_ref,
    col_in,
    lev_in,
    innov_in,
    var_in,
    field_out,
    rows_out,
    sums_ref,
    state,
    courant,
    q0,
    q1,
    q2,
    wind,
    field,
    col_ref,
    lev_ref,
    innov_ref,
    var_ref,
    obs,
    pick,
    held,
    weighted,
    part,
    got,
    red,
    mine,
    more,
    last,
    load_sem,
    halo_send,
    halo_recv,
    obs_send,
    obs_recv,
    pick_send,
    pick_recv,
    rs_send,
    rs_recv,
    ex_send,
    ex_recv,
    ag_send,
    ag_recv,
    out_sem,
):
    tiles = lax.axis_size("tile")
    me = lax.axis_index("member")
    tile = lax.axis_index("tile")
    right = lax.rem(tile + 1, tiles)
    left = lax.rem(tile + tiles - 1, tiles)
    plane_order, depth_order = far_first(plane), far_first(depth)
    a = me * N_Y + (lax.shift_right_logical(tile, 1) & (N_Y - 1))

    def peer(group, r):
        member, shift = offset(group, r)
        return me ^ member, tile ^ shift

    loads = [
        pltpu.make_async_copy(state_ref, state, load_sem.at[0]),
        pltpu.make_async_copy(courant_ref, courant, load_sem.at[1]),
        pltpu.make_async_copy(col_in, col_ref, load_sem.at[2]),
        pltpu.make_async_copy(lev_in, lev_ref, load_sem.at[3]),
        pltpu.make_async_copy(innov_in, innov_ref, load_sem.at[4]),
        pltpu.make_async_copy(var_in, var_ref, load_sem.at[5]),
    ]
    for copy in loads:
        copy.start()

    barrier = pltpu.get_barrier_semaphore()

    def greet(m, t):
        pl.semaphore_signal(barrier, 1, device_id={"member": m, "tile": t}, device_id_type=MESH)

    for other in (left, right):
        greet(me, other)
    for r in depth_order:
        greet(*peer(depth, r))
    for r in plane_order:
        greet(*peer(plane, r))

    for copy in loads[2:]:
        copy.wait()
    obs[me] = jnp.broadcast_to(lev_ref[...] * 1024 + col_ref[...], (8, NOBS))
    for copy in loads[:2]:
        copy.wait()

    def turn(x, _):
        q0[x + 2] = state[pl.ds(x, ROWS, stride=X), :]
        wind[x + 1] = courant[pl.ds(x, 2 * LEV, stride=X), :]
        return 0

    for x in (0, 1, 22, 23):
        turn(x, 0)

    pl.semaphore_wait(barrier, 2 + len(plane_order) + len(depth_order))

    halos = [
        remote(q0.at[pl.ds(X, 2)], q0.at[pl.ds(0, 2)], halo_send.at[0], halo_recv.at[0], me, right),
        remote(wind.at[X], wind.at[0], halo_send.at[1], halo_recv.at[1], me, right),
        remote(q0.at[pl.ds(2, 2)], q0.at[pl.ds(X + 2, 2)], halo_send.at[2], halo_recv.at[2], me, left),
        remote(wind.at[1], wind.at[X + 1], halo_send.at[3], halo_recv.at[3], me, left),
    ]
    for copy in halos:
        copy.start()
    obs_copies = []
    for r in (2, 1, 3):
        to = me ^ r
        copy = remote(obs.at[me], obs.at[me], obs_send.at[r - 1], obs_recv.at[r - 1], to, tile)
        copy.start()
        obs_copies.append(copy)

    lax.fori_loop(2, 22, turn, 0)

    def first(i, _):
        q1[i] = upwind(q0[i + 1], q0[i], q0[i + 2], wind[i])
        return 0

    def second(i, _):
        q2[i] = upwind(q1[i + 1], q1[i], q1[i + 2], wind[i + 1])
        return 0

    def pack(i, _):
        field[pl.ds(i, ROWS, stride=X), :] = q2[i]
        return 0

    lax.fori_loop(2, X, first, 0, unroll=2)
    for copy in halos:
        copy.wait_recv()
    for i in (0, 1, X, X + 1):
        first(i, 0)
    lax.fori_loop(0, X, second, 0, unroll=4)

    outs = [pltpu.make_async_copy(q2, rows_out, out_sem.at[1])]
    outs[0].start()

    for copy in obs_copies:
        copy.wait_recv()

    sub_y = lax.broadcasted_iota(jnp.int32, (CY, NOBS), 0)
    sub_l = lax.broadcasted_iota(jnp.int32, (LEV, NOBS), 0)

    def pick_for(owner):
        code = obs[owner][:1]
        spot = code & 1023
        row = lax.shift_right_logical(code, 10) * 8 + lax.shift_right_logical(spot, 7)
        hot = (sub_y == (spot & 127)).astype(jnp.bfloat16)
        twice = jnp.concatenate([hot, hot], axis=0)
        total = jnp.zeros((LOCAL, LEV, NOBS), jnp.float32)
        for x in range(RUN):
            cells = q2[owner * RUN + x]
            high = cells.astype(jnp.bfloat16)
            rest = cells - high.astype(jnp.float32)
            mid = rest.astype(jnp.bfloat16)
            low = (rest - mid.astype(jnp.float32)).astype(jnp.bfloat16)
            found = jnp.dot(
                jnp.concatenate([high, mid], axis=1), twice, preferred_element_type=jnp.float32
            ) + jnp.dot(low, hot, preferred_element_type=jnp.float32)
            here = (row == sub_l * 8 + x)[None]
            total = total + jnp.where(here, found.reshape(LOCAL, LEV, NOBS), 0.0)
        return jnp.sum(total, axis=1)

    pick_copies = []
    for r in (2, 1, 3):
        to = me ^ r
        pick[r - 1, :LOCAL] = pick_for(to)
        pick[r - 1, LOCAL:] = jnp.zeros((16 - LOCAL, NOBS), jnp.float32)
        copy = remote(pick.at[r - 1], held.at[me], pick_send.at[r - 1], pick_recv.at[r - 1], to, tile)
        copy.start()
        pick_copies.append(copy)
    held[me, :LOCAL] = pick_for(me)
    lax.fori_loop(0, X, pack, 0, unroll=4)
    outs.append(pltpu.make_async_copy(field, field_out, out_sem.at[0]))
    outs[1].start()
    for copy in pick_copies:
        copy.wait_recv()

    picked = jnp.concatenate([held[m][:LOCAL] for m in range(GROUP)], axis=0)
    mean = jnp.sum(picked, axis=0, keepdims=True) * (1.0 / MEMBERS)
    anomaly = (picked - mean) * (1.0 / math.sqrt(MEMBERS - 1.0))
    inverse = 1.0 / var_ref[...]
    scaled = anomaly * inverse
    innov = innov_ref[...] * inverse
    level = lev_ref[...]
    for l in range(LEV):
        at = (l // 3) * 128 + (l % 3) * MEMBERS
        weighted[at : at + MEMBERS] = jnp.where(level == l, scaled, 0.0)
    sub = lax.broadcasted_iota(jnp.int32, (8, NOBS), 0)
    for t in range(6):
        held_here = (level == sub + 3 * t) & (sub < 3)
        weighted[t * 128 + BLOCK : t * 128 + 128] = jnp.where(held_here, innov, 0.0)
    weighted[5 * 128 + MEMBERS : 5 * 128 + BLOCK] = jnp.zeros((BLOCK - MEMBERS, NOBS), jnp.float32)
    sums = lax.dot_general(
        anomaly,
        weighted[...],
        (((1,), (1,)), ((), ())),
        precision=HIGHEST,
        preferred_element_type=jnp.float32,
    )
    for q in range(TILES):
        s, c = q // 6, q % 6
        part[q // piece, (q % piece) * 8 : (q % piece) * 8 + 8] = sums[s * 8 : s * 8 + 8, c * 128 : c * 128 + 128]
    for q in range(TILES, part.shape[0] * piece):
        part[q // piece, (q % piece) * 8 : (q % piece) * 8 + 8] = jnp.zeros((8, 128), jnp.float32)

    def exchange(group, order, source, slots, send, recv):
        for r in order:
            m, t = peer(group, r)
            remote(source(r), slots.at[r - 1], send.at[0], recv.at[0], m, t).start()
        m, t = peer(group, 1)
        whole = remote(slots, slots, send.at[0], recv.at[0], m, t)
        whole.wait_recv()
        return whole

    def tree(values):
        while len(values) > 1:
            values = [values[n] + values[n + 1] for n in range(0, len(values), 2)]
        return values[0]

    sent = [exchange(plane, plane_order, lambda r: part.at[a ^ r], got, rs_send, rs_recv)]
    mine[...] = tree([part[a]] + [got[r] for r in range(len(plane_order))])
    sent.append(exchange(depth, depth_order, lambda r: mine, more, ex_send, ex_recv))
    red[...] = tree([mine[...]] + [more[r] for r in range(len(depth_order))])
    sent.append(exchange(plane, plane_order, lambda r: red, last, ag_send, ag_recv))
    sums_ref[a] = red[...]
    for r in plane_order:
        sums_ref[a ^ r] = last[r - 1]

    for copy in halos + obs_copies + pick_copies + sent:
        copy.wait_send()
    for copy in outs:
        copy.wait()


def dot(left, right):
    return jnp.dot(left, right, precision=HIGHEST, preferred_element_type=jnp.float32)


def solve(piece, sums_ref, waves_ref, field_ref, rows_ref, part_ref, advanced_ref, stack, system, lines, rows, wave_at, power_at, sem):
    me = lax.axis_index("member")
    keep = pltpu.make_async_copy(field_ref, advanced_ref, sem.at[0])
    keep.start()
    load = pltpu.make_async_copy(rows_ref, rows, sem.at[1])
    load.start()

    def iota(shape, axis):
        return lax.broadcasted_iota(jnp.int32, shape, axis)

    waves = [waves_ref[j] for j in range(MODES)]
    for j in range(MODES):
        wave_at[j] = 0
        power_at[j] = 0.0
    count = jnp.int32(0)
    for j in range(MODES):
        power = jnp.float32(0.0)
        fresh = jnp.bool_(True)
        for i in range(MODES):
            same = waves[i] == waves[j]
            power = power + jnp.where(same, 1.0 / (1.0 + i), 0.0)
            if i < j:
                fresh = jnp.logical_and(fresh, jnp.logical_not(same))

        @pl.when(fresh)
        def _(count=count, j=j, power=power):
            wave_at[count] = waves[j]
            power_at[count] = power

        count = count + fresh.astype(jnp.int32)

    def cosines(wave, level):
        turn = (wave * (2 * level + 1)) & 63
        turn = jnp.where(turn > 32, 64 - turn, turn)
        back = turn > 16
        turn = jnp.where(back, 32 - turn, turn)
        angle = turn.astype(jnp.float32) * (math.pi / 32.0)
        square = angle * angle
        value = jnp.full(square.shape, 1.0 / math.factorial(14), jnp.float32)
        for n in (12, 10, 8, 6, 4, 2, 0):
            value = 1.0 / math.factorial(n) - value * square
        return jnp.where(back, -value, value)

    level = iota((LEV, 128), 0)
    lane = iota((LEV, 128), 1)
    columns = []
    for i in range(MODES):
        wave = jnp.full((LEV, 128), wave_at[i], jnp.int32)
        columns.append(jnp.sqrt(jnp.full((LEV, 128), power_at[i], jnp.float32)) * cosines(wave, level))
    across = []
    for c in range(4):
        value = jnp.where(lane < 40, columns[3 * c], jnp.where(lane < 80, columns[3 * c + 1], columns[3 * c + 2]))
        across.append(jnp.where(lane < BLOCK, value, 1.0 if c == 3 else 0.0))

    segment = iota((MEMBERS, 128), 1)
    seg0 = segment < 40
    seg1 = segment < 80
    seg2 = segment < BLOCK
    for t in range(6):
        tile = jnp.concatenate(
            [
                sums_ref[(s * 6 + t) // piece, ((s * 6 + t) % piece) * 8 : ((s * 6 + t) % piece) * 8 + 8]
                for s in range(5)
            ],
            axis=0,
        )
        shifts = {0: tile}
        for d in (1, 2, -1, -2) if t < 5 else (1, 2):
            shifts[d] = pltpu.roll(tile, (40 * d) % 128, 1)
        for u in range(3 if t < 5 else 1):
            last = tile if u == 0 else pltpu.roll(tile, 128 - u, 1)
            stack[3 * t + u] = jnp.where(
                seg0, shifts[-u], jnp.where(seg1, shifts[1 - u], jnp.where(seg2, shifts[2 - u], last))
            )

    row = iota((MEMBERS, 128), 0)
    for i in range(MODES):

        @pl.when(i < count)
        def _(i=i):
            totals = [jnp.zeros((MEMBERS, 128), jnp.float32) for _ in range(4)]
            for c in range(4):
                if c == i // 3:
                    totals[c] = jnp.where(segment == row + 40 * (i % 3), 1.0, 0.0)
            factors = [columns[i] * across[c] for c in range(4)]
            for l in range(LEV):
                gram = stack[l]
                for c in range(4):
                    totals[c] = totals[c] + gram * factors[c][l : l + 1]
            for c in range(4):
                system[i * MEMBERS : (i + 1) * MEMBERS, c * 128 : (c + 1) * 128] = totals[c]

    lines[...] = jnp.zeros(lines.shape, jnp.float32)
    wide = (8, 128)
    sub = iota(wide, 0)

    def spread(x):
        return jnp.broadcast_to(x, wide)

    def clear(s, rows_at, first):
        if rows_at.stop <= rows_at.start:
            return
        c0 = s // 3
        cols = slice(first * 128, 512)
        system[rows_at, cols] = system[rows_at, cols] - dot(
            system[rows_at, c0 * 128 : (c0 + 1) * 128], lines[s % 2, :, cols]
        )

    def deferred(s, first):
        clear(s, slice(0, s * MEMBERS), first)
        clear(s, slice((s + 2) * MEMBERS, MODES * MEMBERS), first)

    def eliminate(s):
        c0, offset = s // 3, (s % 3) * MEMBERS
        tiles = list(range(c0, 4))
        base = s * MEMBERS
        vals = {
            (t, c): system[base + 8 * t : base + 8 * t + 8, c * 128 : (c + 1) * 128] for t in range(5) for c in tiles
        }
        if s > 0:
            deferred(s - 1, c0)
        for p in range(5):
            at = [offset + 8 * p + j for j in range(8)]
            cols = [spread(vals[p, c0][:, a : a + 1]) for a in at]
            others = {
                t: [spread(vals[t, c0][:, a : a + 1]) for a in at] for t in [(p + d) % 5 for d in range(1, 5)]
            }
            pivot = [vals[p, c] for c in tiles]
            for j in range(0, 8, 2):
                c1, c2 = cols[j], cols[j + 1]
                a, b = spread(c1[j : j + 1]), spread(c2[j : j + 1])
                b2, d = spread(c1[j + 1 : j + 2]), spread(c2[j + 1 : j + 2])
                inv = 1.0 / (a * d - b * b2)
                a, b, b2, d = a * inv, b * inv, b2 * inv, d * inv
                s1, s2 = sub == j, sub == j + 1
                m1, m2 = jnp.where(s1 | s2, 0.0, c1), jnp.where(s1 | s2, 0.0, c2)

                def step(v):
                    r1, r2 = spread(v[j : j + 1]), spread(v[j + 1 : j + 2])
                    l1, l2 = d * r1 - b * r2, a * r2 - b2 * r1
                    return jnp.where(s1, l1, jnp.where(s2, l2, v - (m1 * l1 + m2 * l2)))

                cols[j + 2 :] = [step(v) for v in cols[j + 2 :]]
                pivot = [step(v) for v in pivot]
            for n, c in enumerate(tiles):
                vals[p, c] = pivot[n]
                line = [spread(pivot[n][j : j + 1]) for j in range(8)]
                for t, multipliers in others.items():
                    prods = [multipliers[j] * line[j] for j in range(8)]
                    while len(prods) > 1:
                        prods = [prods[k] + prods[k + 1] for k in range(0, len(prods), 2)]
                    vals[t, c] = vals[t, c] - prods[0]
        if s >= 2:
            before = ((s - 2) % 3) * MEMBERS
            lines[s % 2, before : before + MEMBERS] = jnp.zeros((MEMBERS, 512), jnp.float32)
        for (t, c), v in vals.items():
            system[base + 8 * t : base + 8 * t + 8, c * 128 : (c + 1) * 128] = v
            lines[s % 2, offset + 8 * t : offset + 8 * t + 8, c * 128 : (c + 1) * 128] = v
        if s + 1 < MODES:
            clear(s, slice((s + 1) * MEMBERS, (s + 2) * MEMBERS), c0)

    for s in range(MODES):

        @pl.when(s < count)
        def _(s=s):
            eliminate(s)

    for s in range(1, MODES):

        @pl.when(s + 1 == count)
        def _(s=s):
            clear(s, slice(0, s * MEMBERS), 3)

    total = jnp.zeros((LOCAL, LEV, 128), jnp.float32)
    load.wait()
    for i in range(MODES):
        weight = jnp.broadcast_to(
            system[i * MEMBERS : (i + 1) * MEMBERS, 384:512][:, BLOCK : BLOCK + 1], (MEMBERS, 128)
        )
        weight = (weight - jnp.sum(weight, axis=0, keepdims=True) * (1.0 / MEMBERS)) * (
            1.0 / math.sqrt(MEMBERS - 1.0)
        )
        stack[i, :MEMBERS] = weight
    for i in range(MODES):

        @pl.when(i >= count)
        def _(i=i):
            stack[i, :MEMBERS] = jnp.zeros((MEMBERS, 128), jnp.float32)

    parts = []
    for k in range(LOCAL):
        total = jnp.zeros((LEV, 128), jnp.float32)
        for i in range(MODES):
            total = total + columns[i] * stack[i, pl.ds(me * LOCAL + k, 1)]
        parts.append(total)

    def add_up(x, _):
        total = jnp.zeros((LEV, CY), jnp.float32)
        for k in range(LOCAL):
            total = total + rows[x, k * LEV : (k + 1) * LEV] * parts[k]
        part_ref[x] = total
        return 0

    lax.fori_loop(0, X, add_up, 0)
    keep.wait()


def finish(share_ref, out_ref, got, send_sem, recv_sem):
    me = lax.axis_index("member")
    tile = lax.axis_index("tile")
    barrier = pltpu.get_barrier_semaphore()
    for r in (2, 1, 3):
        pl.semaphore_signal(barrier, 1, device_id={"member": me ^ r, "tile": tile}, device_id_type=MESH)
    pl.semaphore_wait(barrier, GROUP - 1)
    copies = []
    for r in (2, 1, 3):
        to = me ^ r
        copy = remote(
            share_ref.at[pl.ds(to * RUN, RUN)], got.at[r - 1], send_sem.at[r - 1], recv_sem.at[r - 1], to, tile
        )
        copy.start()
        copies.append(copy)
    for copy in copies:
        copy.wait_recv()
    for x in range(RUN):
        out_ref[:, x * CY : (x + 1) * CY] = (share_ref[me * RUN + x] + got[0, x]) + (got[1, x] + got[2, x])
    for copy in copies:
        copy.wait_send()


def on_device(member_state, courant, obs_col, obs_lev, innovation, obs_var, mode_waves):
    tiles = lax.axis_size("tile")
    n_z = tiles // (N_Y * N_CORE)
    plane = ((2, None), (N_Y.bit_length() - 1, 1))
    depth = ((n_z.bit_length() - 1, N_Y.bit_length()), (1, 0))
    g1 = GROUP * N_Y
    g2 = n_z * N_CORE
    piece = -(-TILES // g1)
    f32 = jnp.float32
    dma = pltpu.SemaphoreType.DMA
    shape = member_state.shape
    field, rows, sums = pl.pallas_call(
        functools.partial(front, plane, depth, piece),
        out_shape=[
            jax.ShapeDtypeStruct((ROWS * X, CY), f32),
            jax.ShapeDtypeStruct((X, ROWS, CY), f32),
            jax.ShapeDtypeStruct((g1, piece * 8, 128), f32),
        ],
        in_specs=[ANY] * 6,
        out_specs=[ANY, ANY, VMEM],
        scratch_shapes=[
            pltpu.VMEM((ROWS * X, CY), f32),
            pltpu.VMEM((2 * LEV * X, CY), f32),
            pltpu.VMEM((X + 4, ROWS, CY), f32),
            pltpu.VMEM((X + 2, ROWS, CY), f32),
            pltpu.VMEM((X, ROWS, CY), f32),
            pltpu.VMEM((X + 2, 2 * LEV, CY), f32),
            pltpu.VMEM((ROWS * X, CY), f32),
            pltpu.VMEM((1, NOBS), jnp.int32),
            pltpu.VMEM((1, NOBS), jnp.int32),
            pltpu.VMEM((1, NOBS), f32),
            pltpu.VMEM((1, NOBS), f32),
            pltpu.VMEM((GROUP, 8, NOBS), jnp.int32),
            pltpu.VMEM((GROUP - 1, 16, NOBS), f32),
            pltpu.VMEM((GROUP, 16, NOBS), f32),
            pltpu.VMEM((WIDE, NOBS), f32),
            pltpu.VMEM((g1, piece * 8, 128), f32),
            pltpu.VMEM((g1 - 1, piece * 8, 128), f32),
            pltpu.VMEM((piece * 8, 128), f32),
            pltpu.VMEM((piece * 8, 128), f32),
            pltpu.VMEM((g2 - 1, piece * 8, 128), f32),
            pltpu.VMEM((g1 - 1, piece * 8, 128), f32),
            dma((6,)),
            dma((4,)),
            dma((4,)),
            dma((GROUP - 1,)),
            dma((GROUP - 1,)),
            dma((GROUP - 1,)),
            dma((GROUP - 1,)),
            dma((1,)),
            dma((1,)),
            dma((1,)),
            dma((1,)),
            dma((1,)),
            dma((1,)),
            dma((2,)),
        ],
        compiler_params=pltpu.CompilerParams(
            collective_id=0, has_side_effects=True, vmem_limit_bytes=VMEM_LIMIT
        ),
        name="front",
    )(
        member_state.reshape(ROWS * X, CY),
        courant.reshape(2 * LEV * X, CY),
        obs_col.reshape(1, NOBS),
        obs_lev.reshape(1, NOBS),
        innovation.reshape(1, NOBS),
        obs_var.reshape(1, NOBS),
    )
    shares, advanced = pl.pallas_call(
        functools.partial(solve, piece),
        out_shape=[
            jax.ShapeDtypeStruct((X, LEV, CY), f32),
            jax.ShapeDtypeStruct((ROWS * X, CY), f32),
        ],
        in_specs=[VMEM, SMEM, ANY, ANY],
        out_specs=[VMEM, ANY],
        scratch_shapes=[
            pltpu.VMEM((LEV, MEMBERS, 128), f32),
            pltpu.VMEM((MODES * MEMBERS, 512), f32),
            pltpu.VMEM((2, 128, 512), f32),
            pltpu.VMEM((X, ROWS, CY), f32),
            pltpu.SMEM((MODES,), jnp.int32),
            pltpu.SMEM((MODES,), f32),
            dma((2,)),
        ],
        compiler_params=pltpu.CompilerParams(vmem_limit_bytes=VMEM_LIMIT),
        name="solve",
    )(sums, mode_waves, field, rows)
    increment = pl.pallas_call(
        finish,
        out_shape=jax.ShapeDtypeStruct((LEV, RUN * CY), f32),
        in_specs=[VMEM],
        out_specs=VMEM,
        scratch_shapes=[
            pltpu.VMEM((GROUP - 1, RUN, LEV, CY), f32),
            dma((GROUP - 1,)),
            dma((GROUP - 1,)),
        ],
        compiler_params=pltpu.CompilerParams(
            collective_id=1, has_side_effects=True, vmem_limit_bytes=VMEM_LIMIT
        ),
        name="finish",
    )(shares)
    return advanced.reshape(shape), increment


def solution(mesh):
    in_specs = (
        P("member", None, "tile", None),
        P(None, None, "tile", None),
        P(("member", "tile")),
        P(("member", "tile")),
        P(("member", "tile")),
        P(("member", "tile")),
        P(),
    )
    out_specs = (P("member", None, "tile", None), P(None, ("member", "tile")))
    return jax.shard_map(
        on_device, mesh=mesh, in_specs=in_specs, out_specs=out_specs, check_vma=False
    )
```

```python
import functools
import math

import jax
import jax.numpy as jnp
from jax import lax
from jax.experimental import pallas as pl
from jax.experimental.pallas import tpu as pltpu
from jax.sharding import PartitionSpec as P

MESH = pl.DeviceIdType.MESH
HIGHEST = lax.Precision.HIGHEST
ANY = pl.BlockSpec(memory_space=pl.ANY)
VMEM = pl.BlockSpec(memory_space=pltpu.VMEM)
SMEM = pl.BlockSpec(memory_space=pltpu.SMEM)
N_Y = 4
N_CORE = 2
GROUP = 4
LOCAL = 10
MEMBERS = 40
MODES = 12
LEV = 16
X = 24
CY = 128
RUN = 6
ROWS = LOCAL * LEV
NOBS = 512
TILES = 30
BLOCK = 120
WIDE = 768
PANELS = ((0, 1), (2, 3), (4,))
VMEM_LIMIT = 48 * 1024 * 1024


def remote(src, dst, send, recv, member, tile):
    return pltpu.make_async_remote_copy(
        src_ref=src,
        dst_ref=dst,
        send_sem=send,
        recv_sem=recv,
        device_id={"member": member, "tile": tile},
        device_id_type=MESH,
    )


def upwind(centre, west, east, wind):
    cx = wind[:LEV][None]
    cy = wind[LEV:][None]
    lane = lax.broadcasted_iota(jnp.int32, (1, LEV, CY), 2)
    source = jnp.broadcast_to((lane + jnp.where(cy > 0.0, -1, 1)) & (CY - 1), (LOCAL, LEV, CY))
    from_y = jnp.take_along_axis(centre, source.reshape(ROWS, CY), axis=1)
    centre, west, east, from_y = (v.reshape(LOCAL, LEV, CY) for v in (centre, west, east, from_y))
    from_x = jnp.where(cx > 0.0, west, east)
    new = centre - jnp.abs(cx) * (centre - from_x) - jnp.abs(cy) * (centre - from_y)
    return new.reshape(ROWS, CY)


def offset(group, r):
    member = shift = 0
    for bits, place in reversed(group):
        part = r & ((1 << bits) - 1)
        r >>= bits
        if place is None:
            member = part
        else:
            shift |= part << place
    return member, shift


def far_first(group):
    def hops(r):
        total = 0.0
        for bits, place in reversed(group):
            part = r & ((1 << bits) - 1)
            r >>= bits
            if place != 0:
                total += (0.0, 1.0, 2.0, 1.0)[part] if bits == 2 else (0.0, 1.0, 2.0, 2.2, 4.0, 3.0, 2.4, 1.5)[part]
        return total

    count = 1 << sum(bits for bits, _ in group)
    return sorted(range(1, count), key=lambda r: -hops(r))


def front(
    plane,
    depth,
    piece,
    state_ref,
    courant_ref,
    col_in,
    lev_in,
    innov_in,
    var_in,
    field_out,
    rows_out,
    sums_ref,
    state,
    courant,
    q0,
    q1,
    q2,
    wind,
    field,
    col_ref,
    lev_ref,
    innov_ref,
    var_ref,
    obs,
    pick,
    held,
    weighted,
    part,
    got,
    red,
    mine,
    more,
    last,
    load_sem,
    halo_send,
    halo_recv,
    obs_send,
    obs_recv,
    pick_send,
    pick_recv,
    rs_send,
    rs_recv,
    ex_send,
    ex_recv,
    ag_send,
    ag_recv,
    out_sem,
):
    tiles = lax.axis_size("tile")
    me = lax.axis_index("member")
    tile = lax.axis_index("tile")
    right = lax.rem(tile + 1, tiles)
    left = lax.rem(tile + tiles - 1, tiles)
    plane_order, depth_order = far_first(plane), far_first(depth)
    a = me * N_Y + (lax.shift_right_logical(tile, 1) & (N_Y - 1))

    def peer(group, r):
        member, shift = offset(group, r)
        return me ^ member, tile ^ shift

    loads = [
        pltpu.make_async_copy(state_ref, state, load_sem.at[0]),
        pltpu.make_async_copy(courant_ref, courant, load_sem.at[1]),
        pltpu.make_async_copy(col_in, col_ref, load_sem.at[2]),
        pltpu.make_async_copy(lev_in, lev_ref, load_sem.at[3]),
        pltpu.make_async_copy(innov_in, innov_ref, load_sem.at[4]),
        pltpu.make_async_copy(var_in, var_ref, load_sem.at[5]),
    ]
    for copy in loads:
        copy.start()

    barrier = pltpu.get_barrier_semaphore()

    def greet(m, t):
        pl.semaphore_signal(barrier, 1, device_id={"member": m, "tile": t}, device_id_type=MESH)

    for other in (left, right):
        greet(me, other)
    for r in depth_order:
        greet(*peer(depth, r))
    for r in plane_order:
        greet(*peer(plane, r))

    for copy in loads[2:]:
        copy.wait()
    obs[me] = jnp.broadcast_to(lev_ref[...] * 1024 + col_ref[...], (8, NOBS))
    for copy in loads[:2]:
        copy.wait()

    def turn(x, _):
        q0[x + 2] = state[pl.ds(x, ROWS, stride=X), :]
        wind[x + 1] = courant[pl.ds(x, 2 * LEV, stride=X), :]
        return 0

    for x in (0, 1, 22, 23):
        turn(x, 0)

    pl.semaphore_wait(barrier, 2 + len(plane_order) + len(depth_order))

    halos = [
        remote(q0.at[pl.ds(X, 2)], q0.at[pl.ds(0, 2)], halo_send.at[0], halo_recv.at[0], me, right),
        remote(wind.at[X], wind.at[0], halo_send.at[1], halo_recv.at[1], me, right),
        remote(q0.at[pl.ds(2, 2)], q0.at[pl.ds(X + 2, 2)], halo_send.at[2], halo_recv.at[2], me, left),
        remote(wind.at[1], wind.at[X + 1], halo_send.at[3], halo_recv.at[3], me, left),
    ]
    for copy in halos:
        copy.start()
    obs_copies = []
    for r in (2, 1, 3):
        to = me ^ r
        copy = remote(obs.at[me], obs.at[me], obs_send.at[r - 1], obs_recv.at[r - 1], to, tile)
        copy.start()
        obs_copies.append(copy)

    lax.fori_loop(2, 22, turn, 0)

    def first(i, _):
        q1[i] = upwind(q0[i + 1], q0[i], q0[i + 2], wind[i])
        return 0

    def second(i, _):
        q2[i] = upwind(q1[i + 1], q1[i], q1[i + 2], wind[i + 1])
        return 0

    def pack(i, _):
        field[pl.ds(i, ROWS, stride=X), :] = q2[i]
        return 0

    lax.fori_loop(2, X, first, 0, unroll=2)
    for copy in halos:
        copy.wait_recv()
    for i in (0, 1, X, X + 1):
        first(i, 0)
    lax.fori_loop(0, X, second, 0, unroll=4)

    outs = [pltpu.make_async_copy(q2, rows_out, out_sem.at[1])]
    outs[0].start()

    for copy in obs_copies:
        copy.wait_recv()

    sub_y = lax.broadcasted_iota(jnp.int32, (CY, NOBS), 0)
    sub_l = lax.broadcasted_iota(jnp.int32, (LEV, NOBS), 0)

    def pick_for(owner):
        code = obs[owner][:1]
        spot = code & 1023
        row = lax.shift_right_logical(code, 10) * 8 + lax.shift_right_logical(spot, 7)
        hot = (sub_y == (spot & 127)).astype(jnp.bfloat16)
        twice = jnp.concatenate([hot, hot], axis=0)
        total = jnp.zeros((LOCAL, LEV, NOBS), jnp.float32)
        for x in range(RUN):
            cells = q2[owner * RUN + x]
            high = cells.astype(jnp.bfloat16)
            rest = cells - high.astype(jnp.float32)
            mid = rest.astype(jnp.bfloat16)
            low = (rest - mid.astype(jnp.float32)).astype(jnp.bfloat16)
            found = jnp.dot(
                jnp.concatenate([high, mid], axis=1), twice, preferred_element_type=jnp.float32
            ) + jnp.dot(low, hot, preferred_element_type=jnp.float32)
            here = (row == sub_l * 8 + x)[None]
            total = total + jnp.where(here, found.reshape(LOCAL, LEV, NOBS), 0.0)
        return jnp.sum(total, axis=1)

    pick_copies = []
    for r in (2, 1, 3):
        to = me ^ r
        pick[r - 1, :LOCAL] = pick_for(to)
        pick[r - 1, LOCAL:] = jnp.zeros((16 - LOCAL, NOBS), jnp.float32)
        copy = remote(pick.at[r - 1], held.at[me], pick_send.at[r - 1], pick_recv.at[r - 1], to, tile)
        copy.start()
        pick_copies.append(copy)
    held[me, :LOCAL] = pick_for(me)
    lax.fori_loop(0, X, pack, 0, unroll=4)
    outs.append(pltpu.make_async_copy(field, field_out, out_sem.at[0]))
    outs[1].start()
    for copy in pick_copies:
        copy.wait_recv()

    picked = jnp.concatenate([held[m][:LOCAL] for m in range(GROUP)], axis=0)
    mean = jnp.sum(picked, axis=0, keepdims=True) * (1.0 / MEMBERS)
    anomaly = (picked - mean) * (1.0 / math.sqrt(MEMBERS - 1.0))
    inverse = 1.0 / var_ref[...]
    scaled = anomaly * inverse
    innov = innov_ref[...] * inverse
    level = lev_ref[...]
    for l in range(LEV):
        at = (l // 3) * 128 + (l % 3) * MEMBERS
        weighted[at : at + MEMBERS] = jnp.where(level == l, scaled, 0.0)
    sub = lax.broadcasted_iota(jnp.int32, (8, NOBS), 0)
    for t in range(6):
        held_here = (level == sub + 3 * t) & (sub < 3)
        weighted[t * 128 + BLOCK : t * 128 + 128] = jnp.where(held_here, innov, 0.0)
    weighted[5 * 128 + MEMBERS : 5 * 128 + BLOCK] = jnp.zeros((BLOCK - MEMBERS, NOBS), jnp.float32)
    sums = lax.dot_general(
        anomaly,
        weighted[...],
        (((1,), (1,)), ((), ())),
        precision=HIGHEST,
        preferred_element_type=jnp.float32,
    )
    for q in range(TILES):
        s, c = q // 6, q % 6
        part[q // piece, (q % piece) * 8 : (q % piece) * 8 + 8] = sums[s * 8 : s * 8 + 8, c * 128 : c * 128 + 128]
    for q in range(TILES, part.shape[0] * piece):
        part[q // piece, (q % piece) * 8 : (q % piece) * 8 + 8] = jnp.zeros((8, 128), jnp.float32)

    def exchange(group, order, source, slots, send, recv):
        for r in order:
            m, t = peer(group, r)
            remote(source(r), slots.at[r - 1], send.at[0], recv.at[0], m, t).start()
        m, t = peer(group, 1)
        whole = remote(slots, slots, send.at[0], recv.at[0], m, t)
        whole.wait_recv()
        return whole

    def tree(values):
        while len(values) > 1:
            values = [values[n] + values[n + 1] for n in range(0, len(values), 2)]
        return values[0]

    sent = [exchange(plane, plane_order, lambda r: part.at[a ^ r], got, rs_send, rs_recv)]
    mine[...] = tree([part[a]] + [got[r] for r in range(len(plane_order))])
    sent.append(exchange(depth, depth_order, lambda r: mine, more, ex_send, ex_recv))
    red[...] = tree([mine[...]] + [more[r] for r in range(len(depth_order))])
    sent.append(exchange(plane, plane_order, lambda r: red, last, ag_send, ag_recv))
    sums_ref[a] = red[...]
    for r in plane_order:
        sums_ref[a ^ r] = last[r - 1]

    for copy in halos + obs_copies + pick_copies + sent:
        copy.wait_send()
    for copy in outs:
        copy.wait()


def dot(left, right):
    return jnp.dot(left, right, precision=HIGHEST, preferred_element_type=jnp.float32)


def solve(piece, sums_ref, waves_ref, field_ref, coeff_ref, advanced_ref, stack, system, lines, field, wave_at, power_at, sem):
    me = lax.axis_index("member")
    fetch = pltpu.make_async_copy(field_ref, field, sem.at[0])
    fetch.start()

    def iota(shape, axis):
        return lax.broadcasted_iota(jnp.int32, shape, axis)

    waves = [waves_ref[j] for j in range(MODES)]
    for j in range(MODES):
        wave_at[j] = 0
        power_at[j] = 0.0
    count = jnp.int32(0)
    for j in range(MODES):
        power = jnp.float32(0.0)
        fresh = jnp.bool_(True)
        for i in range(MODES):
            same = waves[i] == waves[j]
            power = power + jnp.where(same, 1.0 / (1.0 + i), 0.0)
            if i < j:
                fresh = jnp.logical_and(fresh, jnp.logical_not(same))

        @pl.when(fresh)
        def _(count=count, j=j, power=power):
            wave_at[count] = waves[j]
            power_at[count] = power

        count = count + fresh.astype(jnp.int32)

    def cosines(wave, level):
        turn = (wave * (2 * level + 1)) & 63
        turn = jnp.where(turn > 32, 64 - turn, turn)
        back = turn > 16
        turn = jnp.where(back, 32 - turn, turn)
        angle = turn.astype(jnp.float32) * (math.pi / 32.0)
        square = angle * angle
        value = jnp.full(square.shape, 1.0 / math.factorial(14), jnp.float32)
        for n in (12, 10, 8, 6, 4, 2, 0):
            value = 1.0 / math.factorial(n) - value * square
        return jnp.where(back, -value, value)

    level = iota((LEV, 128), 0)
    lane = iota((LEV, 128), 1)
    columns = []
    for i in range(MODES):
        wave = jnp.full((LEV, 128), wave_at[i], jnp.int32)
        columns.append(jnp.sqrt(jnp.full((LEV, 128), power_at[i], jnp.float32)) * cosines(wave, level))
    across = []
    for c in range(4):
        value = jnp.where(lane < 40, columns[3 * c], jnp.where(lane < 80, columns[3 * c + 1], columns[3 * c + 2]))
        across.append(jnp.where(lane < BLOCK, value, 1.0 if c == 3 else 0.0))

    segment = iota((MEMBERS, 128), 1)
    seg0 = segment < 40
    seg1 = segment < 80
    seg2 = segment < BLOCK
    for t in range(6):
        tile = jnp.concatenate(
            [
                sums_ref[(s * 6 + t) // piece, ((s * 6 + t) % piece) * 8 : ((s * 6 + t) % piece) * 8 + 8]
                for s in range(5)
            ],
            axis=0,
        )
        shifts = {0: tile}
        for d in (1, 2, -1, -2) if t < 5 else (1, 2):
            shifts[d] = pltpu.roll(tile, (40 * d) % 128, 1)
        for u in range(3 if t < 5 else 1):
            last = tile if u == 0 else pltpu.roll(tile, 128 - u, 1)
            stack[3 * t + u] = jnp.where(
                seg0, shifts[-u], jnp.where(seg1, shifts[1 - u], jnp.where(seg2, shifts[2 - u], last))
            )

    row = iota((MEMBERS, 128), 0)
    for i in range(MODES):

        @pl.when(i < count)
        def _(i=i):
            totals = [jnp.zeros((MEMBERS, 128), jnp.float32) for _ in range(4)]
            for c in range(4):
                if c == i // 3:
                    totals[c] = jnp.where(segment == row + 40 * (i % 3), 1.0, 0.0)
            factors = [columns[i] * across[c] for c in range(4)]
            for l in range(LEV):
                gram = stack[l]
                for c in range(4):
                    totals[c] = totals[c] + gram * factors[c][l : l + 1]
            for c in range(4):
                system[i * MEMBERS : (i + 1) * MEMBERS, c * 128 : (c + 1) * 128] = totals[c]

    fetch.wait()
    keep = pltpu.make_async_copy(field, advanced_ref, sem.at[1])
    keep.start()
    lines[...] = jnp.zeros(lines.shape, jnp.float32)
    wide = (8, 128)
    sub = iota(wide, 0)

    def spread(x):
        return jnp.broadcast_to(x, wide)

    def clear(s, rows_at, first):
        if rows_at.stop <= rows_at.start:
            return
        c0 = s // 3
        cols = slice(first * 128, 512)
        system[rows_at, cols] = system[rows_at, cols] - dot(
            system[rows_at, c0 * 128 : (c0 + 1) * 128], lines[s % 2, :, cols]
        )

    def deferred(s, first):
        clear(s, slice(0, s * MEMBERS), first)
        clear(s, slice((s + 2) * MEMBERS, MODES * MEMBERS), first)

    def eliminate(s):
        c0, offset = s // 3, (s % 3) * MEMBERS
        tiles = list(range(c0, 4))
        base = s * MEMBERS
        vals = {
            (t, c): system[base + 8 * t : base + 8 * t + 8, c * 128 : (c + 1) * 128] for t in range(5) for c in tiles
        }
        if s > 0:
            deferred(s - 1, c0)
        for panel in PANELS:
            at = [offset + 8 * panel[0] + j for j in range(8 * len(panel))]
            cols = [{t: spread(vals[t, c0][:, n : n + 1]) for t in panel} for n in at]
            after = [(panel[-1] + d) % 5 for d in range(1, 6 - len(panel))]
            others = {t: [spread(vals[t, c0][:, n : n + 1]) for n in at] for t in after}
            pivot = [{t: vals[t, c] for t in panel} for c in tiles]
            for n in range(0, len(at), 2):
                home, j = panel[n // 8], n % 8
                c1, c2 = cols[n], cols[n + 1]
                a, b = spread(c1[home][j : j + 1]), spread(c2[home][j : j + 1])
                b2, d = spread(c1[home][j + 1 : j + 2]), spread(c2[home][j + 1 : j + 2])
                inv = 1.0 / (a * d - b * b2)
                a, b, b2, d = a * inv, b * inv, b2 * inv, d * inv
                s1, s2 = sub == j, sub == j + 1

                def step(v):
                    r1, r2 = spread(v[home][j : j + 1]), spread(v[home][j + 1 : j + 2])
                    l1, l2 = d * r1 - b * r2, a * r2 - b2 * r1
                    new = {t: v[t] - (c1[t] * l1 + c2[t] * l2) for t in panel}
                    new[home] = jnp.where(s1, l1, jnp.where(s2, l2, new[home]))
                    return new

                cols[n + 2 :] = [step(v) for v in cols[n + 2 :]]
                pivot = [step(v) for v in pivot]
            for n, c in enumerate(tiles):
                line = [spread(pivot[n][panel[j // 8]][j % 8 : j % 8 + 1]) for j in range(len(at))]
                for t in panel:
                    vals[t, c] = pivot[n][t]
                for t, multipliers in others.items():
                    prods = [multipliers[j] * line[j] for j in range(len(at))]
                    while len(prods) > 1:
                        prods = [prods[k] + prods[k + 1] for k in range(0, len(prods), 2)]
                    vals[t, c] = vals[t, c] - prods[0]
        if s >= 2:
            before = ((s - 2) % 3) * MEMBERS
            lines[s % 2, before : before + MEMBERS] = jnp.zeros((MEMBERS, 512), jnp.float32)
        for (t, c), v in vals.items():
            system[base + 8 * t : base + 8 * t + 8, c * 128 : (c + 1) * 128] = v
            lines[s % 2, offset + 8 * t : offset + 8 * t + 8, c * 128 : (c + 1) * 128] = v
        if s + 1 < MODES:
            clear(s, slice((s + 1) * MEMBERS, (s + 2) * MEMBERS), c0)

    for s in range(MODES):

        @pl.when(s < count)
        def _(s=s):
            eliminate(s)

    for s in range(1, MODES):

        @pl.when(s + 1 == count)
        def _(s=s):
            clear(s, slice(0, s * MEMBERS), 3)

    for i in range(MODES):
        weight = jnp.broadcast_to(
            system[i * MEMBERS : (i + 1) * MEMBERS, 384:512][:, BLOCK : BLOCK + 1], (MEMBERS, 128)
        )
        weight = (weight - jnp.sum(weight, axis=0, keepdims=True) * (1.0 / MEMBERS)) * (
            1.0 / math.sqrt(MEMBERS - 1.0)
        )
        stack[i, :MEMBERS] = weight
    for i in range(MODES):

        @pl.when(i >= count)
        def _(i=i):
            stack[i, :MEMBERS] = jnp.zeros((MEMBERS, 128), jnp.float32)

    for k in range(LOCAL):
        total = jnp.zeros((LEV, 128), jnp.float32)
        for i in range(MODES):
            total = total + columns[i] * stack[i, pl.ds(me * LOCAL + k, 1)]
        coeff_ref[k] = total
    keep.wait()


def finish(coeff_ref, rows_ref, out_ref, rows, part, got, load_sem, send_sem, recv_sem):
    me = lax.axis_index("member")
    tile = lax.axis_index("tile")
    barrier = pltpu.get_barrier_semaphore()
    for r in (2, 1, 3):
        pl.semaphore_signal(barrier, 1, device_id={"member": me ^ r, "tile": tile}, device_id_type=MESH)
    load = pltpu.make_async_copy(rows_ref, rows, load_sem)
    load.start()

    def run_for(owner, slot):
        for x in range(RUN):
            total = jnp.zeros((LEV, CY), jnp.float32)
            for k in range(LOCAL):
                total = total + rows[owner * RUN + x, k * LEV : (k + 1) * LEV] * coeff_ref[k]
            part[slot, x] = total

    load.wait()
    copies = []
    for r in (2, 1, 3):
        to = me ^ r
        run_for(to, r)
        if not copies:
            pl.semaphore_wait(barrier, GROUP - 1)
        copy = remote(part.at[r], got.at[r - 1], send_sem.at[r - 1], recv_sem.at[r - 1], to, tile)
        copy.start()
        copies.append(copy)
    run_for(me, 0)
    for copy in copies:
        copy.wait_recv()
    for x in range(RUN):
        out_ref[:, x * CY : (x + 1) * CY] = (part[0, x] + got[0, x]) + (got[1, x] + got[2, x])
    for copy in copies:
        copy.wait_send()


def on_device(member_state, courant, obs_col, obs_lev, innovation, obs_var, mode_waves):
    tiles = lax.axis_size("tile")
    n_z = tiles // (N_Y * N_CORE)
    plane = ((2, None), (N_Y.bit_length() - 1, 1))
    depth = ((n_z.bit_length() - 1, N_Y.bit_length()), (1, 0))
    g1 = GROUP * N_Y
    g2 = n_z * N_CORE
    piece = -(-TILES // g1)
    f32 = jnp.float32
    dma = pltpu.SemaphoreType.DMA
    shape = member_state.shape
    field, rows, sums = pl.pallas_call(
        functools.partial(front, plane, depth, piece),
        out_shape=[
            jax.ShapeDtypeStruct((ROWS * X, CY), f32),
            jax.ShapeDtypeStruct((X, ROWS, CY), f32),
            jax.ShapeDtypeStruct((g1, piece * 8, 128), f32),
        ],
        in_specs=[ANY] * 6,
        out_specs=[ANY, ANY, VMEM],
        scratch_shapes=[
            pltpu.VMEM((ROWS * X, CY), f32),
            pltpu.VMEM((2 * LEV * X, CY), f32),
            pltpu.VMEM((X + 4, ROWS, CY), f32),
            pltpu.VMEM((X + 2, ROWS, CY), f32),
            pltpu.VMEM((X, ROWS, CY), f32),
            pltpu.VMEM((X + 2, 2 * LEV, CY), f32),
            pltpu.VMEM((ROWS * X, CY), f32),
            pltpu.VMEM((1, NOBS), jnp.int32),
            pltpu.VMEM((1, NOBS), jnp.int32),
            pltpu.VMEM((1, NOBS), f32),
            pltpu.VMEM((1, NOBS), f32),
            pltpu.VMEM((GROUP, 8, NOBS), jnp.int32),
            pltpu.VMEM((GROUP - 1, 16, NOBS), f32),
            pltpu.VMEM((GROUP, 16, NOBS), f32),
            pltpu.VMEM((WIDE, NOBS), f32),
            pltpu.VMEM((g1, piece * 8, 128), f32),
            pltpu.VMEM((g1 - 1, piece * 8, 128), f32),
            pltpu.VMEM((piece * 8, 128), f32),
            pltpu.VMEM((piece * 8, 128), f32),
            pltpu.VMEM((g2 - 1, piece * 8, 128), f32),
            pltpu.VMEM((g1 - 1, piece * 8, 128), f32),
            dma((6,)),
            dma((4,)),
            dma((4,)),
            dma((GROUP - 1,)),
            dma((GROUP - 1,)),
            dma((GROUP - 1,)),
            dma((GROUP - 1,)),
            dma((1,)),
            dma((1,)),
            dma((1,)),
            dma((1,)),
            dma((1,)),
            dma((1,)),
            dma((2,)),
        ],
        compiler_params=pltpu.CompilerParams(
            collective_id=0, has_side_effects=True, vmem_limit_bytes=VMEM_LIMIT
        ),
        name="front",
    )(
        member_state.reshape(ROWS * X, CY),
        courant.reshape(2 * LEV * X, CY),
        obs_col.reshape(1, NOBS),
        obs_lev.reshape(1, NOBS),
        innovation.reshape(1, NOBS),
        obs_var.reshape(1, NOBS),
    )
    coeffs, advanced = pl.pallas_call(
        functools.partial(solve, piece),
        out_shape=[
            jax.ShapeDtypeStruct((LOCAL, LEV, CY), f32),
            jax.ShapeDtypeStruct((ROWS * X, CY), f32),
        ],
        in_specs=[VMEM, SMEM, ANY],
        out_specs=[VMEM, ANY],
        scratch_shapes=[
            pltpu.VMEM((LEV, MEMBERS, 128), f32),
            pltpu.VMEM((MODES * MEMBERS, 512), f32),
            pltpu.VMEM((2, 128, 512), f32),
            pltpu.VMEM((ROWS * X, CY), f32),
            pltpu.SMEM((MODES,), jnp.int32),
            pltpu.SMEM((MODES,), f32),
            dma((2,)),
        ],
        compiler_params=pltpu.CompilerParams(vmem_limit_bytes=VMEM_LIMIT),
        name="solve",
    )(sums, mode_waves, field)
    increment = pl.pallas_call(
        finish,
        out_shape=jax.ShapeDtypeStruct((LEV, RUN * CY), f32),
        in_specs=[VMEM, ANY],
        out_specs=VMEM,
        scratch_shapes=[
            pltpu.VMEM((X, ROWS, CY), f32),
            pltpu.VMEM((GROUP, RUN, LEV, CY), f32),
            pltpu.VMEM((GROUP - 1, RUN, LEV, CY), f32),
            dma,
            dma((GROUP - 1,)),
            dma((GROUP - 1,)),
        ],
        compiler_params=pltpu.CompilerParams(
            collective_id=1, has_side_effects=True, vmem_limit_bytes=VMEM_LIMIT
        ),
        name="finish",
    )(coeffs, rows)
    return advanced.reshape(shape), increment


def solution(mesh):
    in_specs = (
        P("member", None, "tile", None),
        P(None, None, "tile", None),
        P(("member", "tile")),
        P(("member", "tile")),
        P(("member", "tile")),
        P(("member", "tile")),
        P(),
    )
    out_specs = (P("member", None, "tile", None), P(None, ("member", "tile")))
    return jax.shard_map(
        on_device, mesh=mesh, in_specs=in_specs, out_specs=out_specs, check_vma=False
    )
```

```python
import functools
import math

import jax
import jax.numpy as jnp
from jax import lax
from jax.experimental import pallas as pl
from jax.experimental.pallas import tpu as pltpu
from jax.sharding import PartitionSpec as P

MESH = pl.DeviceIdType.MESH
HIGHEST = lax.Precision.HIGHEST
ANY = pl.BlockSpec(memory_space=pl.ANY)
VMEM = pl.BlockSpec(memory_space=pltpu.VMEM)
SMEM = pl.BlockSpec(memory_space=pltpu.SMEM)
N_Y = 4
N_CORE = 2
GROUP = 4
LOCAL = 10
MEMBERS = 40
MODES = 12
LEV = 16
X = 24
CY = 128
RUN = 6
ROWS = LOCAL * LEV
NOBS = 512
TILES = 30
BLOCK = 120
WIDE = 768
AHEAD = 8
PANELS = ((0,), (1,), (2,), (3,), (4,))
FRONT_VMEM = 56 * 1024 * 1024
SOLVE_VMEM = 53 * 1024 * 1024
FINISH_VMEM = 52 * 1024 * 1024


def remote(src, dst, send, recv, member, tile):
    return pltpu.make_async_remote_copy(
        src_ref=src,
        dst_ref=dst,
        send_sem=send,
        recv_sem=recv,
        device_id={"member": member, "tile": tile},
        device_id_type=MESH,
    )


def upwind(centre, west, east, wind):
    cx = wind[:LEV][None]
    cy = wind[LEV:][None]
    lane = lax.broadcasted_iota(jnp.int32, (1, LEV, CY), 2)
    source = jnp.broadcast_to((lane + jnp.where(cy > 0.0, -1, 1)) & (CY - 1), (LOCAL, LEV, CY))
    from_y = jnp.take_along_axis(centre, source.reshape(ROWS, CY), axis=1)
    centre, west, east, from_y = (v.reshape(LOCAL, LEV, CY) for v in (centre, west, east, from_y))
    from_x = jnp.where(cx > 0.0, west, east)
    new = centre - jnp.abs(cx) * (centre - from_x) - jnp.abs(cy) * (centre - from_y)
    return new.reshape(ROWS, CY)


def offset(group, r):
    member = shift = 0
    for bits, place in reversed(group):
        part = r & ((1 << bits) - 1)
        r >>= bits
        if place is None:
            member = part
        else:
            shift |= part << place
    return member, shift


def far_first(group):
    def hops(r):
        total = 0.0
        for bits, place in reversed(group):
            part = r & ((1 << bits) - 1)
            r >>= bits
            if place != 0:
                total += (0.0, 1.0, 2.0, 1.0)[part] if bits == 2 else (0.0, 1.0, 2.0, 2.2, 4.0, 3.0, 2.4, 1.5)[part]
        return total

    count = 1 << sum(bits for bits, _ in group)
    return sorted(range(1, count), key=lambda r: -hops(r))


def front(
    plane,
    depth,
    piece,
    state_ref,
    courant_ref,
    col_in,
    lev_in,
    innov_in,
    var_in,
    field_out,
    rows_out,
    sums_ref,
    state,
    courant,
    q0,
    q1,
    q2,
    wind,
    field,
    col_ref,
    lev_ref,
    innov_ref,
    var_ref,
    obs,
    pick,
    held,
    weighted,
    part,
    got,
    red,
    mine,
    more,
    last,
    load_sem,
    halo_send,
    halo_recv,
    obs_send,
    obs_recv,
    pick_send,
    pick_recv,
    rs_send,
    rs_recv,
    ex_send,
    ex_recv,
    ag_send,
    ag_recv,
    out_sem,
):
    tiles = lax.axis_size("tile")
    me = lax.axis_index("member")
    tile = lax.axis_index("tile")
    right = lax.rem(tile + 1, tiles)
    left = lax.rem(tile + tiles - 1, tiles)
    plane_order, depth_order = far_first(plane), far_first(depth)
    a = me * N_Y + (lax.shift_right_logical(tile, 1) & (N_Y - 1))

    def peer(group, r):
        member, shift = offset(group, r)
        return me ^ member, tile ^ shift

    loads = [
        pltpu.make_async_copy(state_ref, state, load_sem.at[0]),
        pltpu.make_async_copy(courant_ref, courant, load_sem.at[1]),
        pltpu.make_async_copy(col_in, col_ref, load_sem.at[2]),
        pltpu.make_async_copy(lev_in, lev_ref, load_sem.at[3]),
        pltpu.make_async_copy(innov_in, innov_ref, load_sem.at[4]),
        pltpu.make_async_copy(var_in, var_ref, load_sem.at[5]),
    ]
    for copy in loads:
        copy.start()

    barrier = pltpu.get_barrier_semaphore()

    def greet(m, t):
        pl.semaphore_signal(barrier, 1, device_id={"member": m, "tile": t}, device_id_type=MESH)

    for other in (left, right):
        greet(me, other)
    for r in depth_order:
        greet(*peer(depth, r))
    for r in plane_order:
        greet(*peer(plane, r))

    for copy in loads[2:]:
        copy.wait()
    obs[me] = jnp.broadcast_to(lev_ref[...] * 1024 + col_ref[...], (8, NOBS))
    for copy in loads[:2]:
        copy.wait()

    def turn(x, _):
        q0[x + 2] = state[pl.ds(x, ROWS, stride=X), :]
        wind[x + 1] = courant[pl.ds(x, 2 * LEV, stride=X), :]
        return 0

    for x in (0, 1, 22, 23):
        turn(x, 0)

    pl.semaphore_wait(barrier, 2 + len(plane_order) + len(depth_order))

    halos = [
        remote(q0.at[pl.ds(X, 2)], q0.at[pl.ds(0, 2)], halo_send.at[0], halo_recv.at[0], me, right),
        remote(wind.at[X], wind.at[0], halo_send.at[1], halo_recv.at[1], me, right),
        remote(q0.at[pl.ds(2, 2)], q0.at[pl.ds(X + 2, 2)], halo_send.at[2], halo_recv.at[2], me, left),
        remote(wind.at[1], wind.at[X + 1], halo_send.at[3], halo_recv.at[3], me, left),
    ]
    for copy in halos:
        copy.start()
    obs_copies = []
    for r in (2, 1, 3):
        to = me ^ r
        copy = remote(obs.at[me], obs.at[me], obs_send.at[r - 1], obs_recv.at[r - 1], to, tile)
        copy.start()
        obs_copies.append(copy)

    lax.fori_loop(2, 22, turn, 0)

    def first(i, _):
        q1[i] = upwind(q0[i + 1], q0[i], q0[i + 2], wind[i])
        return 0

    def second(i, _):
        q2[i] = upwind(q1[i + 1], q1[i], q1[i + 2], wind[i + 1])
        return 0

    def pack(i, _):
        field[pl.ds(i, ROWS, stride=X), :] = q2[i]
        return 0

    for i in (2, X - 1):
        first(i, 0)
    lax.fori_loop(3, X - 1, first, 0, unroll=4)
    lax.fori_loop(2, X - 2, second, 0, unroll=4)
    for copy in halos:
        copy.wait_recv()
    for i in (0, 1, X, X + 1):
        first(i, 0)
    for i in (0, 1, X - 2, X - 1):
        second(i, 0)

    outs = [pltpu.make_async_copy(q2, rows_out, out_sem.at[1])]
    outs[0].start()

    for copy in obs_copies:
        copy.wait_recv()

    sub_y = lax.broadcasted_iota(jnp.int32, (CY, NOBS), 0)
    sub_l = lax.broadcasted_iota(jnp.int32, (LEV, NOBS), 0)

    def pick_for(owner):
        code = obs[owner][:1]
        spot = code & 1023
        row = lax.shift_right_logical(code, 10) * 8 + lax.shift_right_logical(spot, 7)
        hot = (sub_y == (spot & 127)).astype(jnp.bfloat16)
        twice = jnp.concatenate([hot, hot], axis=0)
        total = jnp.zeros((LOCAL, LEV, NOBS), jnp.float32)
        for x in range(RUN):
            cells = q2[owner * RUN + x]
            high = cells.astype(jnp.bfloat16)
            rest = cells - high.astype(jnp.float32)
            mid = rest.astype(jnp.bfloat16)
            low = (rest - mid.astype(jnp.float32)).astype(jnp.bfloat16)
            found = jnp.dot(
                jnp.concatenate([high, mid], axis=1), twice, preferred_element_type=jnp.float32
            ) + jnp.dot(low, hot, preferred_element_type=jnp.float32)
            here = (row == sub_l * 8 + x)[None]
            total = total + jnp.where(here, found.reshape(LOCAL, LEV, NOBS), 0.0)
        return jnp.sum(total, axis=1)

    pick_copies = []
    for r in (2, 1, 3):
        to = me ^ r
        pick[r - 1, :LOCAL] = pick_for(to)
        pick[r - 1, LOCAL:] = jnp.zeros((16 - LOCAL, NOBS), jnp.float32)
        copy = remote(pick.at[r - 1], held.at[me], pick_send.at[r - 1], pick_recv.at[r - 1], to, tile)
        copy.start()
        pick_copies.append(copy)
    held[me, :LOCAL] = pick_for(me)
    lax.fori_loop(0, X, pack, 0, unroll=4)
    outs.append(pltpu.make_async_copy(field, field_out, out_sem.at[0]))
    outs[1].start()
    for copy in pick_copies:
        copy.wait_recv()

    picked = jnp.concatenate([held[m][:LOCAL] for m in range(GROUP)], axis=0)
    mean = jnp.sum(picked, axis=0, keepdims=True) * (1.0 / MEMBERS)
    anomaly = (picked - mean) * (1.0 / math.sqrt(MEMBERS - 1.0))
    inverse = 1.0 / var_ref[...]
    scaled = anomaly * inverse
    innov = innov_ref[...] * inverse
    level = lev_ref[...]
    for l in range(LEV):
        at = (l // 3) * 128 + (l % 3) * MEMBERS
        weighted[at : at + MEMBERS] = jnp.where(level == l, scaled, 0.0)
    sub = lax.broadcasted_iota(jnp.int32, (8, NOBS), 0)
    for t in range(6):
        held_here = (level == sub + 3 * t) & (sub < 3)
        weighted[t * 128 + BLOCK : t * 128 + 128] = jnp.where(held_here, innov, 0.0)
    weighted[5 * 128 + MEMBERS : 5 * 128 + BLOCK] = jnp.zeros((BLOCK - MEMBERS, NOBS), jnp.float32)
    sums = lax.dot_general(
        anomaly,
        weighted[...],
        (((1,), (1,)), ((), ())),
        precision=HIGHEST,
        preferred_element_type=jnp.float32,
    )
    for q in range(TILES):
        s, c = q // 6, q % 6
        part[q // piece, (q % piece) * 8 : (q % piece) * 8 + 8] = sums[s * 8 : s * 8 + 8, c * 128 : c * 128 + 128]
    for q in range(TILES, part.shape[0] * piece):
        part[q // piece, (q % piece) * 8 : (q % piece) * 8 + 8] = jnp.zeros((8, 128), jnp.float32)

    def exchange(group, order, source, slots, send, recv):
        for r in order:
            m, t = peer(group, r)
            remote(source(r), slots.at[r - 1], send.at[0], recv.at[0], m, t).start()
        m, t = peer(group, 1)
        whole = remote(slots, slots, send.at[0], recv.at[0], m, t)
        whole.wait_recv()
        return whole

    def tree(values):
        while len(values) > 1:
            values = [values[n] + values[n + 1] for n in range(0, len(values), 2)]
        return values[0]

    sent = [exchange(plane, plane_order, lambda r: part.at[a ^ r], got, rs_send, rs_recv)]
    mine[...] = tree([part[a]] + [got[r] for r in range(len(plane_order))])
    sent.append(exchange(depth, depth_order, lambda r: mine, more, ex_send, ex_recv))
    red[...] = tree([mine[...]] + [more[r] for r in range(len(depth_order))])
    sent.append(exchange(plane, plane_order, lambda r: red, last, ag_send, ag_recv))
    sums_ref[a] = red[...]
    for r in plane_order:
        sums_ref[a ^ r] = last[r - 1]

    for copy in halos + obs_copies + pick_copies + sent:
        copy.wait_send()
    for copy in outs:
        copy.wait()


def dot(left, right):
    return jnp.dot(left, right, precision=HIGHEST, preferred_element_type=jnp.float32)


def solve(piece, sums_in, waves_ref, field_ref, coeff_ref, advanced_ref, sums_ref, stack, system, lines, field, wave_at, power_at, sem):
    me = lax.axis_index("member")
    take = pltpu.make_async_copy(sums_in, sums_ref, sem.at[2])
    take.start()
    fetch = pltpu.make_async_copy(field_ref, field, sem.at[0])
    fetch.start()

    def iota(shape, axis):
        return lax.broadcasted_iota(jnp.int32, shape, axis)

    waves = [waves_ref[j] for j in range(MODES)]
    for j in range(MODES):
        wave_at[j] = 0
        power_at[j] = 0.0
    count = jnp.int32(0)
    for j in range(MODES):
        power = jnp.float32(0.0)
        fresh = jnp.bool_(True)
        for i in range(MODES):
            same = waves[i] == waves[j]
            power = power + jnp.where(same, 1.0 / (1.0 + i), 0.0)
            if i < j:
                fresh = jnp.logical_and(fresh, jnp.logical_not(same))

        @pl.when(fresh)
        def _(count=count, j=j, power=power):
            wave_at[count] = waves[j]
            power_at[count] = power

        count = count + fresh.astype(jnp.int32)

    def cosines(wave, level):
        turn = (wave * (2 * level + 1)) & 63
        turn = jnp.where(turn > 32, 64 - turn, turn)
        back = turn > 16
        turn = jnp.where(back, 32 - turn, turn)
        angle = turn.astype(jnp.float32) * (math.pi / 32.0)
        square = angle * angle
        value = jnp.full(square.shape, 1.0 / math.factorial(14), jnp.float32)
        for n in (12, 10, 8, 6, 4, 2, 0):
            value = 1.0 / math.factorial(n) - value * square
        return jnp.where(back, -value, value)

    level = iota((LEV, 128), 0)
    lane = iota((LEV, 128), 1)
    columns = []
    for i in range(MODES):
        wave = jnp.full((LEV, 128), wave_at[i], jnp.int32)
        columns.append(jnp.sqrt(jnp.full((LEV, 128), power_at[i], jnp.float32)) * cosines(wave, level))
    across = []
    for c in range(4):
        value = jnp.where(lane < 40, columns[3 * c], jnp.where(lane < 80, columns[3 * c + 1], columns[3 * c + 2]))
        across.append(jnp.where(lane < BLOCK, value, 1.0 if c == 3 else 0.0))

    segment = iota((MEMBERS, 128), 1)
    seg0 = segment < 40
    seg1 = segment < 80
    seg2 = segment < BLOCK
    take.wait()
    for t in range(6):
        tile = jnp.concatenate(
            [
                sums_ref[(s * 6 + t) // piece, ((s * 6 + t) % piece) * 8 : ((s * 6 + t) % piece) * 8 + 8]
                for s in range(5)
            ],
            axis=0,
        )
        shifts = {0: tile}
        for d in (1, 2, -1, -2) if t < 5 else (1, 2):
            shifts[d] = pltpu.roll(tile, (40 * d) % 128, 1)
        for u in range(3 if t < 5 else 1):
            last = tile if u == 0 else pltpu.roll(tile, 128 - u, 1)
            stack[3 * t + u] = jnp.where(
                seg0, shifts[-u], jnp.where(seg1, shifts[1 - u], jnp.where(seg2, shifts[2 - u], last))
            )

    row = iota((MEMBERS, 128), 0)
    for i in range(MODES):

        @pl.when(i < count)
        def _(i=i):
            totals = [jnp.zeros((MEMBERS, 128), jnp.float32) for _ in range(4)]
            for c in range(4):
                if c == i // 3:
                    totals[c] = jnp.where(segment == row + 40 * (i % 3), 1.0, 0.0)
            factors = [columns[i] * across[c] for c in range(4)]
            for l in range(LEV):
                gram = stack[l]
                for c in range(4):
                    totals[c] = totals[c] + gram * factors[c][l : l + 1]
            for c in range(4):
                system[i * MEMBERS : (i + 1) * MEMBERS, c * 128 : (c + 1) * 128] = totals[c]

    fetch.wait()
    keep = pltpu.make_async_copy(field, advanced_ref, sem.at[1])
    keep.start()
    lines[...] = jnp.zeros(lines.shape, jnp.float32)
    wide = (8, 128)
    sub = iota(wide, 0)

    def spread(x):
        return jnp.broadcast_to(x, wide)

    def clear(s, rows_at, first):
        if rows_at.stop <= rows_at.start:
            return
        c0 = s // 3
        cols = slice(first * 128, 512)
        system[rows_at, cols] = system[rows_at, cols] - dot(
            system[rows_at, c0 * 128 : (c0 + 1) * 128], lines[s % 2, :, cols]
        )

    def deferred(s, first):
        edges = [(s + 1) * MEMBERS + AHEAD, (s + 2) * MEMBERS, (s + 3) * MEMBERS, MODES * MEMBERS]
        for start, stop in zip(edges[:-1], edges[1:]):
            clear(s, slice(start, min(stop, MODES * MEMBERS)), first)
        clear(s, slice(0, s * MEMBERS), first)

    def eliminate(s):
        c0, offset = s // 3, (s % 3) * MEMBERS
        tiles = list(range(c0, 4))
        base = s * MEMBERS
        extra = list(range(5, 5 + AHEAD // 8)) if s + 1 < MODES else []

        def spot(t, c):
            return slice(base + 8 * t, base + 8 * t + 8), slice(c * 128, (c + 1) * 128)

        if s >= 2:
            before = ((s - 2) % 3) * MEMBERS
            lines[s % 2, before : before + MEMBERS] = jnp.zeros((MEMBERS, 512), jnp.float32)
        if s > 0:
            deferred(s - 1, c0)
        for panel in PANELS:
            at = [offset + 8 * panel[0] + j for j in range(8 * len(panel))]
            pivot = [{t: system[spot(t, c)] for t in panel} for c in tiles]
            cols = [{t: spread(pivot[0][t][:, n : n + 1]) for t in panel} for n in at]
            after = [(panel[-1] + d) % 5 for d in range(1, 6 - len(panel))] + extra
            for n in range(0, len(at), 2):
                home, j = panel[n // 8], n % 8
                c1, c2 = cols[n], cols[n + 1]
                a, b = spread(c1[home][j : j + 1]), spread(c2[home][j : j + 1])
                b2, d = spread(c1[home][j + 1 : j + 2]), spread(c2[home][j + 1 : j + 2])
                inv = 1.0 / (a * d - b * b2)
                a, b, b2, d = a * inv, b * inv, b2 * inv, d * inv
                s1, s2 = sub == j, sub == j + 1

                def step(v):
                    r1, r2 = spread(v[home][j : j + 1]), spread(v[home][j + 1 : j + 2])
                    l1, l2 = d * r1 - b * r2, a * r2 - b2 * r1
                    new = {t: v[t] - (c1[t] * l1 + c2[t] * l2) for t in panel}
                    new[home] = jnp.where(s1, l1, jnp.where(s2, l2, new[home]))
                    return new

                cols[n + 2 :] = [step(v) for v in cols[n + 2 :]]
                pivot = [step(v) for v in pivot]
            line = {}
            for n, c in enumerate(tiles):
                for t in panel:
                    system[spot(t, c)] = pivot[n][t]
                for j in range(len(at)):
                    line[c, j] = spread(pivot[n][panel[j // 8]][j % 8 : j % 8 + 1])
            for t in after:
                head = system[spot(t, c0)]
                multipliers = [spread(head[:, n : n + 1]) for n in at]
                for c in tiles:
                    prods = [multipliers[j] * line[c, j] for j in range(len(at))]
                    while len(prods) > 1:
                        prods = [prods[k] + prods[k + 1] for k in range(0, len(prods), 2)]
                    system[spot(t, c)] = system[spot(t, c)] - prods[0]
        for t in range(5):
            for c in tiles:
                lines[s % 2, offset + 8 * t : offset + 8 * t + 8, c * 128 : (c + 1) * 128] = system[spot(t, c)]

    for s in range(MODES):

        @pl.when(s < count)
        def _(s=s):
            eliminate(s)

    for s in range(1, MODES):

        @pl.when(s + 1 == count)
        def _(s=s):
            clear(s, slice(0, s * MEMBERS), 3)

    for i in range(MODES):
        weight = jnp.broadcast_to(
            system[i * MEMBERS : (i + 1) * MEMBERS, 384:512][:, BLOCK : BLOCK + 1], (MEMBERS, 128)
        )
        weight = (weight - jnp.sum(weight, axis=0, keepdims=True) * (1.0 / MEMBERS)) * (
            1.0 / math.sqrt(MEMBERS - 1.0)
        )
        stack[i, :MEMBERS] = weight
    for i in range(MODES):

        @pl.when(i >= count)
        def _(i=i):
            stack[i, :MEMBERS] = jnp.zeros((MEMBERS, 128), jnp.float32)

    for k in range(LOCAL):
        total = jnp.zeros((LEV, 128), jnp.float32)
        for i in range(MODES):
            total = total + columns[i] * stack[i, pl.ds(me * LOCAL + k, 1)]
        coeff_ref[k] = total
    keep.wait()


def finish(coeff_in, rows_ref, out_ref, coeff_ref, rows, part, got, load_sem, send_sem, recv_sem):
    me = lax.axis_index("member")
    tile = lax.axis_index("tile")
    barrier = pltpu.get_barrier_semaphore()
    for r in (2, 1, 3):
        pl.semaphore_signal(barrier, 1, device_id={"member": me ^ r, "tile": tile}, device_id_type=MESH)
    loads = [
        pltpu.make_async_copy(rows_ref, rows, load_sem.at[0]),
        pltpu.make_async_copy(coeff_in, coeff_ref, load_sem.at[1]),
    ]
    for copy in loads:
        copy.start()

    def run_for(owner, slot):
        for x in range(RUN):
            total = jnp.zeros((LEV, CY), jnp.float32)
            for k in range(LOCAL):
                total = total + rows[owner * RUN + x, k * LEV : (k + 1) * LEV] * coeff_ref[k]
            part[slot, x] = total

    for copy in loads:
        copy.wait()
    copies = []
    for r in (2, 1, 3):
        to = me ^ r
        run_for(to, r)
        if not copies:
            pl.semaphore_wait(barrier, GROUP - 1)
        copy = remote(part.at[r], got.at[r - 1], send_sem.at[r - 1], recv_sem.at[r - 1], to, tile)
        copy.start()
        copies.append(copy)
    run_for(me, 0)
    for copy in copies:
        copy.wait_recv()
    for x in range(RUN):
        out_ref[:, x * CY : (x + 1) * CY] = (part[0, x] + got[0, x]) + (got[1, x] + got[2, x])
    for copy in copies:
        copy.wait_send()


def on_device(member_state, courant, obs_col, obs_lev, innovation, obs_var, mode_waves):
    tiles = lax.axis_size("tile")
    n_z = tiles // (N_Y * N_CORE)
    plane = ((2, None), (N_Y.bit_length() - 1, 1))
    depth = ((n_z.bit_length() - 1, N_Y.bit_length()), (1, 0))
    g1 = GROUP * N_Y
    g2 = n_z * N_CORE
    piece = -(-TILES // g1)
    f32 = jnp.float32
    dma = pltpu.SemaphoreType.DMA
    shape = member_state.shape
    field, rows, sums = pl.pallas_call(
        functools.partial(front, plane, depth, piece),
        out_shape=[
            jax.ShapeDtypeStruct((ROWS * X, CY), f32),
            jax.ShapeDtypeStruct((X, ROWS, CY), f32),
            jax.ShapeDtypeStruct((g1, piece * 8, 128), f32),
        ],
        in_specs=[ANY] * 6,
        out_specs=[ANY, ANY, VMEM],
        scratch_shapes=[
            pltpu.VMEM((ROWS * X, CY), f32),
            pltpu.VMEM((2 * LEV * X, CY), f32),
            pltpu.VMEM((X + 4, ROWS, CY), f32),
            pltpu.VMEM((X + 2, ROWS, CY), f32),
            pltpu.VMEM((X, ROWS, CY), f32),
            pltpu.VMEM((X + 2, 2 * LEV, CY), f32),
            pltpu.VMEM((ROWS * X, CY), f32),
            pltpu.VMEM((1, NOBS), jnp.int32),
            pltpu.VMEM((1, NOBS), jnp.int32),
            pltpu.VMEM((1, NOBS), f32),
            pltpu.VMEM((1, NOBS), f32),
            pltpu.VMEM((GROUP, 8, NOBS), jnp.int32),
            pltpu.VMEM((GROUP - 1, 16, NOBS), f32),
            pltpu.VMEM((GROUP, 16, NOBS), f32),
            pltpu.VMEM((WIDE, NOBS), f32),
            pltpu.VMEM((g1, piece * 8, 128), f32),
            pltpu.VMEM((g1 - 1, piece * 8, 128), f32),
            pltpu.VMEM((piece * 8, 128), f32),
            pltpu.VMEM((piece * 8, 128), f32),
            pltpu.VMEM((g2 - 1, piece * 8, 128), f32),
            pltpu.VMEM((g1 - 1, piece * 8, 128), f32),
            dma((6,)),
            dma((4,)),
            dma((4,)),
            dma((GROUP - 1,)),
            dma((GROUP - 1,)),
            dma((GROUP - 1,)),
            dma((GROUP - 1,)),
            dma((1,)),
            dma((1,)),
            dma((1,)),
            dma((1,)),
            dma((1,)),
            dma((1,)),
            dma((2,)),
        ],
        compiler_params=pltpu.CompilerParams(
            collective_id=0, has_side_effects=True, vmem_limit_bytes=FRONT_VMEM
        ),
        name="front",
    )(
        member_state.reshape(ROWS * X, CY),
        courant.reshape(2 * LEV * X, CY),
        obs_col.reshape(1, NOBS),
        obs_lev.reshape(1, NOBS),
        innovation.reshape(1, NOBS),
        obs_var.reshape(1, NOBS),
    )
    coeffs, advanced = pl.pallas_call(
        functools.partial(solve, piece),
        out_shape=[
            jax.ShapeDtypeStruct((LOCAL, LEV, CY), f32),
            jax.ShapeDtypeStruct((ROWS * X, CY), f32),
        ],
        in_specs=[ANY, SMEM, ANY],
        out_specs=[VMEM, ANY],
        scratch_shapes=[
            pltpu.VMEM(sums.shape, f32),
            pltpu.VMEM((LEV, MEMBERS, 128), f32),
            pltpu.VMEM((MODES * MEMBERS, 512), f32),
            pltpu.VMEM((2, 128, 512), f32),
            pltpu.VMEM((ROWS * X, CY), f32),
            pltpu.SMEM((MODES,), jnp.int32),
            pltpu.SMEM((MODES,), f32),
            dma((3,)),
        ],
        compiler_params=pltpu.CompilerParams(vmem_limit_bytes=SOLVE_VMEM),
        name="solve",
    )(sums, mode_waves, field)
    increment = pl.pallas_call(
        finish,
        out_shape=jax.ShapeDtypeStruct((LEV, RUN * CY), f32),
        in_specs=[ANY, ANY],
        out_specs=VMEM,
        scratch_shapes=[
            pltpu.VMEM((LOCAL, LEV, CY), f32),
            pltpu.VMEM((X, ROWS, CY), f32),
            pltpu.VMEM((GROUP, RUN, LEV, CY), f32),
            pltpu.VMEM((GROUP - 1, RUN, LEV, CY), f32),
            dma((2,)),
            dma((GROUP - 1,)),
            dma((GROUP - 1,)),
        ],
        compiler_params=pltpu.CompilerParams(
            collective_id=1, has_side_effects=True, vmem_limit_bytes=FINISH_VMEM
        ),
        name="finish",
    )(coeffs, rows)
    return advanced.reshape(shape), increment


def solution(mesh):
    in_specs = (
        P("member", None, "tile", None),
        P(None, None, "tile", None),
        P(("member", "tile")),
        P(("member", "tile")),
        P(("member", "tile")),
        P(("member", "tile")),
        P(),
    )
    out_specs = (P("member", None, "tile", None), P(None, ("member", "tile")))
    return jax.shard_map(
        on_device, mesh=mesh, in_specs=in_specs, out_specs=out_specs, check_vma=False
    )
```

```python
import functools
import math

import jax
import jax.numpy as jnp
from jax import lax
from jax.experimental import pallas as pl
from jax.experimental.pallas import tpu as pltpu
from jax.sharding import PartitionSpec as P

MESH = pl.DeviceIdType.MESH
HIGHEST = lax.Precision.HIGHEST
ANY = pl.BlockSpec(memory_space=pl.ANY)
VMEM = pl.BlockSpec(memory_space=pltpu.VMEM)
SMEM = pl.BlockSpec(memory_space=pltpu.SMEM)
N_Y = 4
N_CORE = 2
GROUP = 4
LOCAL = 10
MEMBERS = 40
MODES = 12
LEV = 16
X = 24
CY = 128
RUN = 6
ROWS = LOCAL * LEV
NOBS = 512
TILES = 30
BLOCK = 120
WIDE = 768
AHEAD = 8
FRONT_VMEM = 56 * 1024 * 1024
SOLVE_VMEM = 53 * 1024 * 1024
FINISH_VMEM = 52 * 1024 * 1024


def remote(src, dst, send, recv, member, tile):
    return pltpu.make_async_remote_copy(
        src_ref=src,
        dst_ref=dst,
        send_sem=send,
        recv_sem=recv,
        device_id={"member": member, "tile": tile},
        device_id_type=MESH,
    )


def upwind(centre, west, east, wind):
    cx = wind[:LEV][None]
    cy = wind[LEV:][None]
    lane = lax.broadcasted_iota(jnp.int32, (1, LEV, CY), 2)
    source = jnp.broadcast_to((lane + jnp.where(cy > 0.0, -1, 1)) & (CY - 1), (LOCAL, LEV, CY))
    from_y = jnp.take_along_axis(centre, source.reshape(ROWS, CY), axis=1)
    centre, west, east, from_y = (v.reshape(LOCAL, LEV, CY) for v in (centre, west, east, from_y))
    from_x = jnp.where(cx > 0.0, west, east)
    new = centre - jnp.abs(cx) * (centre - from_x) - jnp.abs(cy) * (centre - from_y)
    return new.reshape(ROWS, CY)


def offset(group, r):
    member = shift = 0
    for bits, place in reversed(group):
        part = r & ((1 << bits) - 1)
        r >>= bits
        if place is None:
            member = part
        else:
            shift |= part << place
    return member, shift


def far_first(group):
    def hops(r):
        total = 0.0
        for bits, place in reversed(group):
            part = r & ((1 << bits) - 1)
            r >>= bits
            if place != 0:
                total += (0.0, 1.0, 2.0, 1.0)[part] if bits == 2 else (0.0, 1.0, 2.0, 2.2, 4.0, 3.0, 2.4, 1.5)[part]
        return total

    count = 1 << sum(bits for bits, _ in group)
    return sorted(range(1, count), key=lambda r: -hops(r))


def front(
    plane,
    depth,
    piece,
    state_ref,
    courant_ref,
    col_in,
    lev_in,
    innov_in,
    var_in,
    field_out,
    rows_out,
    sums_out,
    state,
    courant,
    q0,
    q1,
    q2,
    wind,
    field,
    col_ref,
    lev_ref,
    innov_ref,
    var_ref,
    obs,
    pick,
    held,
    weighted,
    part,
    got,
    red,
    mine,
    more,
    last,
    sums_ref,
    load_sem,
    halo_send,
    halo_recv,
    obs_send,
    obs_recv,
    pick_send,
    pick_recv,
    rs_send,
    rs_recv,
    ex_send,
    ex_recv,
    ag_send,
    ag_recv,
    out_sem,
):
    tiles = lax.axis_size("tile")
    me = lax.axis_index("member")
    tile = lax.axis_index("tile")
    right = lax.rem(tile + 1, tiles)
    left = lax.rem(tile + tiles - 1, tiles)
    plane_order, depth_order = far_first(plane), far_first(depth)
    a = me * N_Y + (lax.shift_right_logical(tile, 1) & (N_Y - 1))

    def peer(group, r):
        member, shift = offset(group, r)
        return me ^ member, tile ^ shift

    loads = [
        pltpu.make_async_copy(state_ref, state, load_sem.at[0]),
        pltpu.make_async_copy(courant_ref, courant, load_sem.at[1]),
        pltpu.make_async_copy(col_in, col_ref, load_sem.at[2]),
        pltpu.make_async_copy(lev_in, lev_ref, load_sem.at[3]),
        pltpu.make_async_copy(innov_in, innov_ref, load_sem.at[4]),
        pltpu.make_async_copy(var_in, var_ref, load_sem.at[5]),
    ]
    for copy in loads:
        copy.start()

    barrier = pltpu.get_barrier_semaphore()

    def greet(m, t):
        pl.semaphore_signal(barrier, 1, device_id={"member": m, "tile": t}, device_id_type=MESH)

    for other in (left, right):
        greet(me, other)
    for r in depth_order:
        greet(*peer(depth, r))
    for r in plane_order:
        greet(*peer(plane, r))

    for copy in loads[2:]:
        copy.wait()
    obs[me] = jnp.broadcast_to(lev_ref[...] * 1024 + col_ref[...], (8, NOBS))
    for copy in loads[:2]:
        copy.wait()

    def turn(x, _):
        q0[x + 2] = state[pl.ds(x, ROWS, stride=X), :]
        wind[x + 1] = courant[pl.ds(x, 2 * LEV, stride=X), :]
        return 0

    for x in (0, 1, 22, 23):
        turn(x, 0)

    pl.semaphore_wait(barrier, 2 + len(plane_order) + len(depth_order))

    halos = [
        remote(q0.at[pl.ds(X, 2)], q0.at[pl.ds(0, 2)], halo_send.at[0], halo_recv.at[0], me, right),
        remote(wind.at[X], wind.at[0], halo_send.at[1], halo_recv.at[1], me, right),
        remote(q0.at[pl.ds(2, 2)], q0.at[pl.ds(X + 2, 2)], halo_send.at[2], halo_recv.at[2], me, left),
        remote(wind.at[1], wind.at[X + 1], halo_send.at[3], halo_recv.at[3], me, left),
    ]
    for copy in halos:
        copy.start()
    obs_copies = []
    for r in (2, 1, 3):
        to = me ^ r
        copy = remote(obs.at[me], obs.at[me], obs_send.at[r - 1], obs_recv.at[r - 1], to, tile)
        copy.start()
        obs_copies.append(copy)

    lax.fori_loop(2, 22, turn, 0, unroll=5)

    def first(i, _):
        q1[i] = upwind(q0[i + 1], q0[i], q0[i + 2], wind[i])
        return 0

    def second(i, _):
        q2[i] = upwind(q1[i + 1], q1[i], q1[i + 2], wind[i + 1])
        return 0

    def pack(i, _):
        field[pl.ds(i, ROWS, stride=X), :] = q2[i]
        return 0

    for i in (2, X - 1):
        first(i, 0)
    lax.fori_loop(3, X - 1, first, 0, unroll=20)
    lax.fori_loop(2, X - 2, second, 0, unroll=20)
    for copy in halos:
        copy.wait_recv()
    for i in (0, 1, X, X + 1):
        first(i, 0)
    for i in (0, 1, X - 2, X - 1):
        second(i, 0)

    outs = [pltpu.make_async_copy(q2, rows_out, out_sem.at[1])]
    outs[0].start()

    for copy in obs_copies:
        copy.wait_recv()

    sub_y = lax.broadcasted_iota(jnp.int32, (CY, NOBS), 0)
    sub_l = lax.broadcasted_iota(jnp.int32, (LEV, NOBS), 0)

    def pick_for(owner):
        code = obs[owner][:1]
        spot = code & 1023
        row = lax.shift_right_logical(code, 10) * 8 + lax.shift_right_logical(spot, 7)
        hot = (sub_y == (spot & 127)).astype(jnp.bfloat16)
        twice = jnp.concatenate([hot, hot], axis=0)
        total = jnp.zeros((LOCAL, LEV, NOBS), jnp.float32)
        for x in range(RUN):
            cells = q2[owner * RUN + x]
            high = cells.astype(jnp.bfloat16)
            rest = cells - high.astype(jnp.float32)
            mid = rest.astype(jnp.bfloat16)
            low = (rest - mid.astype(jnp.float32)).astype(jnp.bfloat16)
            found = jnp.dot(
                jnp.concatenate([high, mid], axis=1), twice, preferred_element_type=jnp.float32
            ) + jnp.dot(low, hot, preferred_element_type=jnp.float32)
            here = (row == sub_l * 8 + x)[None]
            total = total + jnp.where(here, found.reshape(LOCAL, LEV, NOBS), 0.0)
        return jnp.sum(total, axis=1)

    pick_copies = []
    for r in (2, 1, 3):
        to = me ^ r
        pick[r - 1, :LOCAL] = pick_for(to)
        pick[r - 1, LOCAL:] = jnp.zeros((16 - LOCAL, NOBS), jnp.float32)
        copy = remote(pick.at[r - 1], held.at[me], pick_send.at[r - 1], pick_recv.at[r - 1], to, tile)
        copy.start()
        pick_copies.append(copy)
    held[me, :LOCAL] = pick_for(me)
    lax.fori_loop(0, X, pack, 0, unroll=4)
    outs.append(pltpu.make_async_copy(field, field_out, out_sem.at[0]))
    outs[1].start()
    for copy in pick_copies:
        copy.wait_recv()

    picked = jnp.concatenate([held[m][:LOCAL] for m in range(GROUP)], axis=0)
    mean = jnp.sum(picked, axis=0, keepdims=True) * (1.0 / MEMBERS)
    anomaly = (picked - mean) * (1.0 / math.sqrt(MEMBERS - 1.0))
    inverse = 1.0 / var_ref[...]
    scaled = anomaly * inverse
    innov = innov_ref[...] * inverse
    level = lev_ref[...]
    for l in range(LEV):
        at = (l // 3) * 128 + (l % 3) * MEMBERS
        weighted[at : at + MEMBERS] = jnp.where(level == l, scaled, 0.0)
    sub = lax.broadcasted_iota(jnp.int32, (8, NOBS), 0)
    for t in range(6):
        held_here = (level == sub + 3 * t) & (sub < 3)
        weighted[t * 128 + BLOCK : t * 128 + 128] = jnp.where(held_here, innov, 0.0)
    weighted[5 * 128 + MEMBERS : 5 * 128 + BLOCK] = jnp.zeros((BLOCK - MEMBERS, NOBS), jnp.float32)
    sums = lax.dot_general(
        anomaly,
        weighted[...],
        (((1,), (1,)), ((), ())),
        precision=HIGHEST,
        preferred_element_type=jnp.float32,
    )
    for q in range(TILES):
        s, c = q // 6, q % 6
        part[q // piece, (q % piece) * 8 : (q % piece) * 8 + 8] = sums[s * 8 : s * 8 + 8, c * 128 : c * 128 + 128]
    for q in range(TILES, part.shape[0] * piece):
        part[q // piece, (q % piece) * 8 : (q % piece) * 8 + 8] = jnp.zeros((8, 128), jnp.float32)

    def exchange(group, order, source, slots, send, recv):
        for r in order:
            m, t = peer(group, r)
            remote(source(r), slots.at[r - 1], send.at[0], recv.at[0], m, t).start()
        m, t = peer(group, 1)
        whole = remote(slots, slots, send.at[0], recv.at[0], m, t)
        whole.wait_recv()
        return whole

    def tree(values):
        while len(values) > 1:
            values = [values[n] + values[n + 1] for n in range(0, len(values), 2)]
        return values[0]

    sent = [exchange(plane, plane_order, lambda r: part.at[a ^ r], got, rs_send, rs_recv)]
    mine[...] = tree([part[a]] + [got[r] for r in range(len(plane_order))])
    sent.append(exchange(depth, depth_order, lambda r: mine, more, ex_send, ex_recv))
    red[...] = tree([mine[...]] + [more[r] for r in range(len(depth_order))])
    sent.append(exchange(plane, plane_order, lambda r: red, last, ag_send, ag_recv))
    sums_ref[a] = red[...]
    for r in plane_order:
        sums_ref[a ^ r] = last[r - 1]
    outs.append(pltpu.make_async_copy(sums_ref, sums_out.at[pl.ds(0, sums_ref.shape[0])], out_sem.at[2]))
    outs[2].start()

    for copy in halos + obs_copies + pick_copies + sent:
        copy.wait_send()
    for copy in outs:
        copy.wait()


def dot(left, right):
    return jnp.dot(left, right, precision=HIGHEST, preferred_element_type=jnp.float32)


def solve(piece, sums_in, waves_ref, field_ref, coeff_ref, advanced_ref, sums_ref, stack, system, lines, field, wave_at, power_at, sem):
    me = lax.axis_index("member")
    take = pltpu.make_async_copy(sums_in.at[pl.ds(0, sums_ref.shape[0])], sums_ref, sem.at[2])
    take.start()
    fetch = pltpu.make_async_copy(field_ref, field, sem.at[0])
    fetch.start()

    def iota(shape, axis):
        return lax.broadcasted_iota(jnp.int32, shape, axis)

    waves = [waves_ref[j] for j in range(MODES)]
    for j in range(MODES):
        wave_at[j] = 0
        power_at[j] = 0.0
    count = jnp.int32(0)
    for j in range(MODES):
        power = jnp.float32(0.0)
        fresh = jnp.bool_(True)
        for i in range(MODES):
            same = waves[i] == waves[j]
            power = power + jnp.where(same, 1.0 / (1.0 + i), 0.0)
            if i < j:
                fresh = jnp.logical_and(fresh, jnp.logical_not(same))

        @pl.when(fresh)
        def _(count=count, j=j, power=power):
            wave_at[count] = waves[j]
            power_at[count] = power

        count = count + fresh.astype(jnp.int32)

    def cosines(wave, level):
        turn = (wave * (2 * level + 1)) & 63
        turn = jnp.where(turn > 32, 64 - turn, turn)
        back = turn > 16
        turn = jnp.where(back, 32 - turn, turn)
        angle = turn.astype(jnp.float32) * (math.pi / 32.0)
        square = angle * angle
        value = jnp.full(square.shape, 1.0 / math.factorial(14), jnp.float32)
        for n in (12, 10, 8, 6, 4, 2, 0):
            value = 1.0 / math.factorial(n) - value * square
        return jnp.where(back, -value, value)

    level = iota((LEV, 128), 0)
    lane = iota((LEV, 128), 1)
    columns = []
    for i in range(MODES):
        wave = jnp.full((LEV, 128), wave_at[i], jnp.int32)
        columns.append(jnp.sqrt(jnp.full((LEV, 128), power_at[i], jnp.float32)) * cosines(wave, level))
    across = []
    for c in range(4):
        value = jnp.where(lane < 40, columns[3 * c], jnp.where(lane < 80, columns[3 * c + 1], columns[3 * c + 2]))
        across.append(jnp.where(lane < BLOCK, value, 1.0 if c == 3 else 0.0))

    segment = iota((MEMBERS, 128), 1)
    seg0 = segment < 40
    seg1 = segment < 80
    seg2 = segment < BLOCK
    take.wait()
    for t in range(6):
        tile = jnp.concatenate(
            [
                sums_ref[(s * 6 + t) // piece, ((s * 6 + t) % piece) * 8 : ((s * 6 + t) % piece) * 8 + 8]
                for s in range(5)
            ],
            axis=0,
        )
        shifts = {0: tile}
        for d in (1, 2, -1, -2) if t < 5 else (1, 2):
            shifts[d] = pltpu.roll(tile, (40 * d) % 128, 1)
        for u in range(3 if t < 5 else 1):
            last = tile if u == 0 else pltpu.roll(tile, 128 - u, 1)
            stack[3 * t + u] = jnp.where(
                seg0, shifts[-u], jnp.where(seg1, shifts[1 - u], jnp.where(seg2, shifts[2 - u], last))
            )

    row = iota((MEMBERS, 128), 0)
    for i in range(MODES):

        @pl.when(i < count)
        def _(i=i):
            totals = [jnp.zeros((MEMBERS, 128), jnp.float32) for _ in range(4)]
            for c in range(4):
                if c == i // 3:
                    totals[c] = jnp.where(segment == row + 40 * (i % 3), 1.0, 0.0)
            factors = [columns[i] * across[c] for c in range(4)]
            for l in range(LEV):
                gram = stack[l]
                for c in range(4):
                    totals[c] = totals[c] + gram * factors[c][l : l + 1]
            for c in range(4):
                system[i * MEMBERS : (i + 1) * MEMBERS, c * 128 : (c + 1) * 128] = totals[c]

    fetch.wait()
    keep = pltpu.make_async_copy(field, advanced_ref, sem.at[1])
    keep.start()
    lines[...] = jnp.zeros(lines.shape, jnp.float32)
    wide = (8, 128)
    sub = iota(wide, 0)

    def spread(x):
        return jnp.broadcast_to(x, wide)

    def clear(s, rows_at, first):
        if rows_at.stop <= rows_at.start:
            return
        c0 = s // 3
        cols = slice(first * 128, 512)
        system[rows_at, cols] = system[rows_at, cols] - dot(
            system[rows_at, c0 * 128 : (c0 + 1) * 128], lines[s % 2, :, cols]
        )

    def deferred(s, first):
        edges = [(s + 1) * MEMBERS + AHEAD, (s + 2) * MEMBERS, (s + 3) * MEMBERS, MODES * MEMBERS]
        for start, stop in zip(edges[:-1], edges[1:]):
            clear(s, slice(start, min(stop, MODES * MEMBERS)), first)
        clear(s, slice(0, s * MEMBERS), first)

    def eliminate(s):
        c0, offset = s // 3, (s % 3) * MEMBERS
        tiles = list(range(c0, 4))
        base = s * MEMBERS
        extra = list(range(5, 5 + AHEAD // 8)) if s + 1 < MODES else []

        def spot(t, c):
            return slice(base + 8 * t, base + 8 * t + 8), slice(c * 128, (c + 1) * 128)

        if s >= 2:
            before = ((s - 2) % 3) * MEMBERS
            lines[s % 2, before : before + MEMBERS] = jnp.zeros((MEMBERS, 512), jnp.float32)
        if s > 0:
            deferred(s - 1, c0)
        for p in range(5):
            at = [offset + 8 * p + j for j in range(8)]
            pivot = [system[spot(p, c)] for c in tiles]
            cols = [spread(pivot[0][:, n : n + 1]) for n in at]
            keep_row = swap_row = jnp.zeros(wide, jnp.float32)
            for j in range(0, 8, 2):
                c1, c2 = cols[j], cols[j + 1]
                a, b = spread(c1[j : j + 1]), spread(c2[j : j + 1])
                b2, d = spread(c1[j + 1 : j + 2]), spread(c2[j + 1 : j + 2])
                inv = 1.0 / (a * d - b * b2)
                s1, s2 = sub == j, sub == j + 1
                m1 = jnp.where(s1 | s2, 0.0, c1 * d - c2 * b2) * inv
                m2 = jnp.where(s1 | s2, 0.0, c2 * a - c1 * b) * inv
                keep_row = jnp.where(s1, d * inv, jnp.where(s2, a * inv, keep_row))
                swap_row = jnp.where(s1, b * inv, jnp.where(s2, b2 * inv, swap_row))

                def step(v):
                    return v - (m1 * spread(v[j : j + 1]) + m2 * spread(v[j + 1 : j + 2]))

                cols[j + 2 :] = [step(v) for v in cols[j + 2 :]]
                pivot = [step(v) for v in pivot]
            line = {}
            for n, c in enumerate(tiles):
                v = pivot[n]
                swapped = jnp.where(sub % 2 == 0, pltpu.roll(v, 7, 0), pltpu.roll(v, 1, 0))
                v = keep_row * v - swap_row * swapped
                system[spot(p, c)] = v
                for j in range(8):
                    line[c, j] = spread(v[j : j + 1])
            for t in [(p + d) % 5 for d in range(1, 5)] + extra:
                head = system[spot(t, c0)]
                multipliers = [spread(head[:, n : n + 1]) for n in at]
                for c in tiles:
                    prods = [multipliers[j] * line[c, j] for j in range(8)]
                    while len(prods) > 1:
                        prods = [prods[k] + prods[k + 1] for k in range(0, len(prods), 2)]
                    system[spot(t, c)] = system[spot(t, c)] - prods[0]
        for t in range(5):
            for c in tiles:
                lines[s % 2, offset + 8 * t : offset + 8 * t + 8, c * 128 : (c + 1) * 128] = system[spot(t, c)]

    for s in range(MODES):

        @pl.when(s < count)
        def _(s=s):
            eliminate(s)

    for s in range(1, MODES):

        @pl.when(s + 1 == count)
        def _(s=s):
            clear(s, slice(0, s * MEMBERS), 3)

    for i in range(MODES):
        weight = jnp.broadcast_to(
            system[i * MEMBERS : (i + 1) * MEMBERS, 384:512][:, BLOCK : BLOCK + 1], (MEMBERS, 128)
        )
        weight = (weight - jnp.sum(weight, axis=0, keepdims=True) * (1.0 / MEMBERS)) * (
            1.0 / math.sqrt(MEMBERS - 1.0)
        )
        stack[i, :MEMBERS] = weight
    for i in range(MODES):

        @pl.when(i >= count)
        def _(i=i):
            stack[i, :MEMBERS] = jnp.zeros((MEMBERS, 128), jnp.float32)

    for k in range(LOCAL):
        total = jnp.zeros((LEV, 128), jnp.float32)
        for i in range(MODES):
            total = total + columns[i] * stack[i, pl.ds(me * LOCAL + k, 1)]
        coeff_ref[k] = total
    keep.wait()


def finish(coeff_in, rows_ref, out_ref, coeff_ref, rows, part, got, load_sem, send_sem, recv_sem):
    me = lax.axis_index("member")
    tile = lax.axis_index("tile")
    barrier = pltpu.get_barrier_semaphore()
    for r in (2, 1, 3):
        pl.semaphore_signal(barrier, 1, device_id={"member": me ^ r, "tile": tile}, device_id_type=MESH)
    loads = [
        pltpu.make_async_copy(rows_ref, rows, load_sem.at[0]),
        pltpu.make_async_copy(coeff_in, coeff_ref, load_sem.at[1]),
    ]
    for copy in loads:
        copy.start()

    def run_for(owner, slot):
        for x in range(RUN):
            total = jnp.zeros((LEV, CY), jnp.float32)
            for k in range(LOCAL):
                total = total + rows[owner * RUN + x, k * LEV : (k + 1) * LEV] * coeff_ref[k]
            part[slot, x] = total

    for copy in loads:
        copy.wait()
    copies = []
    for r in (2, 1, 3):
        to = me ^ r
        run_for(to, r)
        if not copies:
            pl.semaphore_wait(barrier, GROUP - 1)
        copy = remote(part.at[r], got.at[r - 1], send_sem.at[r - 1], recv_sem.at[r - 1], to, tile)
        copy.start()
        copies.append(copy)
    run_for(me, 0)
    for copy in copies:
        copy.wait_recv()
    for x in range(RUN):
        out_ref[:, x * CY : (x + 1) * CY] = (part[0, x] + got[0, x]) + (got[1, x] + got[2, x])
    for copy in copies:
        copy.wait_send()


def on_device(member_state, courant, obs_col, obs_lev, innovation, obs_var, mode_waves):
    tiles = lax.axis_size("tile")
    n_z = tiles // (N_Y * N_CORE)
    plane = ((2, None), (N_Y.bit_length() - 1, 1))
    depth = ((n_z.bit_length() - 1, N_Y.bit_length()), (1, 0))
    g1 = GROUP * N_Y
    g2 = n_z * N_CORE
    piece = -(-TILES // g1)
    f32 = jnp.float32
    dma = pltpu.SemaphoreType.DMA
    shape = member_state.shape
    field, rows, sums = pl.pallas_call(
        functools.partial(front, plane, depth, piece),
        out_shape=[
            jax.ShapeDtypeStruct((ROWS * X, CY), f32),
            jax.ShapeDtypeStruct((X, ROWS, CY), f32),
            jax.ShapeDtypeStruct((16 * g1, piece * 8, 128), f32),
        ],
        in_specs=[ANY] * 6,
        out_specs=[ANY, ANY, ANY],
        scratch_shapes=[
            pltpu.VMEM((ROWS * X, CY), f32),
            pltpu.VMEM((2 * LEV * X, CY), f32),
            pltpu.VMEM((X + 4, ROWS, CY), f32),
            pltpu.VMEM((X + 2, ROWS, CY), f32),
            pltpu.VMEM((X, ROWS, CY), f32),
            pltpu.VMEM((X + 2, 2 * LEV, CY), f32),
            pltpu.VMEM((ROWS * X, CY), f32),
            pltpu.VMEM((1, NOBS), jnp.int32),
            pltpu.VMEM((1, NOBS), jnp.int32),
            pltpu.VMEM((1, NOBS), f32),
            pltpu.VMEM((1, NOBS), f32),
            pltpu.VMEM((GROUP, 8, NOBS), jnp.int32),
            pltpu.VMEM((GROUP - 1, 16, NOBS), f32),
            pltpu.VMEM((GROUP, 16, NOBS), f32),
            pltpu.VMEM((WIDE, NOBS), f32),
            pltpu.VMEM((g1, piece * 8, 128), f32),
            pltpu.VMEM((g1 - 1, piece * 8, 128), f32),
            pltpu.VMEM((piece * 8, 128), f32),
            pltpu.VMEM((piece * 8, 128), f32),
            pltpu.VMEM((g2 - 1, piece * 8, 128), f32),
            pltpu.VMEM((g1 - 1, piece * 8, 128), f32),
            pltpu.VMEM((g1, piece * 8, 128), f32),
            dma((6,)),
            dma((4,)),
            dma((4,)),
            dma((GROUP - 1,)),
            dma((GROUP - 1,)),
            dma((GROUP - 1,)),
            dma((GROUP - 1,)),
            dma((1,)),
            dma((1,)),
            dma((1,)),
            dma((1,)),
            dma((1,)),
            dma((1,)),
            dma((3,)),
        ],
        compiler_params=pltpu.CompilerParams(
            collective_id=0, has_side_effects=True, vmem_limit_bytes=FRONT_VMEM
        ),
        name="front",
    )(
        member_state.reshape(ROWS * X, CY),
        courant.reshape(2 * LEV * X, CY),
        obs_col.reshape(1, NOBS),
        obs_lev.reshape(1, NOBS),
        innovation.reshape(1, NOBS),
        obs_var.reshape(1, NOBS),
    )
    coeffs, advanced = pl.pallas_call(
        functools.partial(solve, piece),
        out_shape=[
            jax.ShapeDtypeStruct((LOCAL, LEV, CY), f32),
            jax.ShapeDtypeStruct((ROWS * X, CY), f32),
        ],
        in_specs=[ANY, SMEM, ANY],
        out_specs=[VMEM, ANY],
        scratch_shapes=[
            pltpu.VMEM((g1, piece * 8, 128), f32),
            pltpu.VMEM((LEV, MEMBERS, 128), f32),
            pltpu.VMEM((MODES * MEMBERS, 512), f32),
            pltpu.VMEM((2, 128, 512), f32),
            pltpu.VMEM((ROWS * X, CY), f32),
            pltpu.SMEM((MODES,), jnp.int32),
            pltpu.SMEM((MODES,), f32),
            dma((3,)),
        ],
        compiler_params=pltpu.CompilerParams(vmem_limit_bytes=SOLVE_VMEM),
        name="solve",
    )(sums, mode_waves, field)
    increment = pl.pallas_call(
        finish,
        out_shape=jax.ShapeDtypeStruct((LEV, RUN * CY), f32),
        in_specs=[ANY, ANY],
        out_specs=VMEM,
        scratch_shapes=[
            pltpu.VMEM((LOCAL, LEV, CY), f32),
            pltpu.VMEM((X, ROWS, CY), f32),
            pltpu.VMEM((GROUP, RUN, LEV, CY), f32),
            pltpu.VMEM((GROUP - 1, RUN, LEV, CY), f32),
            dma((2,)),
            dma((GROUP - 1,)),
            dma((GROUP - 1,)),
        ],
        compiler_params=pltpu.CompilerParams(
            collective_id=1, has_side_effects=True, vmem_limit_bytes=FINISH_VMEM
        ),
        name="finish",
    )(coeffs, rows)
    return advanced.reshape(shape), increment


def solution(mesh):
    in_specs = (
        P("member", None, "tile", None),
        P(None, None, "tile", None),
        P(("member", "tile")),
        P(("member", "tile")),
        P(("member", "tile")),
        P(("member", "tile")),
        P(),
    )
    out_specs = (P("member", None, "tile", None), P(None, ("member", "tile")))
    return jax.shard_map(
        on_device, mesh=mesh, in_specs=in_specs, out_specs=out_specs, check_vma=False
    )
```

```python
import functools
import math

import jax
import jax.numpy as jnp
from jax import lax
from jax.experimental import pallas as pl
from jax.experimental.pallas import tpu as pltpu
from jax.sharding import PartitionSpec as P

MESH = pl.DeviceIdType.MESH
HIGHEST = lax.Precision.HIGHEST
ANY = pl.BlockSpec(memory_space=pl.ANY)
VMEM = pl.BlockSpec(memory_space=pltpu.VMEM)
SMEM = pl.BlockSpec(memory_space=pltpu.SMEM)
N_Y = 4
N_CORE = 2
GROUP = 4
LOCAL = 10
MEMBERS = 40
MODES = 12
LEV = 16
X = 24
CY = 128
RUN = 6
ROWS = LOCAL * LEV
NOBS = 512
TILES = 30
BLOCK = 120
WIDE = 768
AHEAD = 8
FRONT_VMEM = 56 * 1024 * 1024
SOLVE_VMEM = 53 * 1024 * 1024
FINISH_VMEM = 52 * 1024 * 1024


def remote(src, dst, send, recv, member, tile):
    return pltpu.make_async_remote_copy(
        src_ref=src,
        dst_ref=dst,
        send_sem=send,
        recv_sem=recv,
        device_id={"member": member, "tile": tile},
        device_id_type=MESH,
    )


def upwind(centre, west, east, wind):
    cx = wind[:LEV][None]
    cy = wind[LEV:][None]
    lane = lax.broadcasted_iota(jnp.int32, (1, LEV, CY), 2)
    source = jnp.broadcast_to((lane + jnp.where(cy > 0.0, -1, 1)) & (CY - 1), (LOCAL, LEV, CY))
    from_y = jnp.take_along_axis(centre, source.reshape(ROWS, CY), axis=1)
    centre, west, east, from_y = (v.reshape(LOCAL, LEV, CY) for v in (centre, west, east, from_y))
    from_x = jnp.where(cx > 0.0, west, east)
    new = centre - jnp.abs(cx) * (centre - from_x) - jnp.abs(cy) * (centre - from_y)
    return new.reshape(ROWS, CY)


def offset(group, r):
    member = shift = 0
    for bits, place in reversed(group):
        part = r & ((1 << bits) - 1)
        r >>= bits
        if place is None:
            member = part
        else:
            shift |= part << place
    return member, shift


def far_first(group):
    def hops(r):
        total = 0.0
        for bits, place in reversed(group):
            part = r & ((1 << bits) - 1)
            r >>= bits
            if place != 0:
                total += (0.0, 1.0, 2.0, 1.0)[part] if bits == 2 else (0.0, 1.0, 2.0, 2.2, 4.0, 3.0, 2.4, 1.5)[part]
        return total

    count = 1 << sum(bits for bits, _ in group)
    return sorted(range(1, count), key=lambda r: -hops(r))


def front(
    plane,
    depth,
    piece,
    state_ref,
    courant_ref,
    col_in,
    lev_in,
    innov_in,
    var_in,
    field_out,
    rows_out,
    sums_out,
    state,
    courant,
    q0,
    q1,
    q2,
    wind,
    field,
    col_ref,
    lev_ref,
    innov_ref,
    var_ref,
    obs,
    pick,
    held,
    weighted,
    part,
    got,
    red,
    mine,
    more,
    last,
    sums_ref,
    load_sem,
    halo_send,
    halo_recv,
    obs_send,
    obs_recv,
    pick_send,
    pick_recv,
    rs_send,
    rs_recv,
    ex_send,
    ex_recv,
    ag_send,
    ag_recv,
    out_sem,
):
    tiles = lax.axis_size("tile")
    me = lax.axis_index("member")
    tile = lax.axis_index("tile")
    right = lax.rem(tile + 1, tiles)
    left = lax.rem(tile + tiles - 1, tiles)
    plane_order, depth_order = far_first(plane), far_first(depth)
    a = me * N_Y + (lax.shift_right_logical(tile, 1) & (N_Y - 1))

    def peer(group, r):
        member, shift = offset(group, r)
        return me ^ member, tile ^ shift

    loads = [
        pltpu.make_async_copy(state_ref, state.at[pl.ds(0, ROWS * X)], load_sem.at[0]),
        pltpu.make_async_copy(courant_ref, courant.at[pl.ds(0, 2 * LEV * X)], load_sem.at[1]),
        pltpu.make_async_copy(col_in, col_ref, load_sem.at[2]),
        pltpu.make_async_copy(lev_in, lev_ref, load_sem.at[3]),
        pltpu.make_async_copy(innov_in, innov_ref, load_sem.at[4]),
        pltpu.make_async_copy(var_in, var_ref, load_sem.at[5]),
    ]
    for copy in loads:
        copy.start()

    barrier = pltpu.get_barrier_semaphore()

    def greet(m, t):
        pl.semaphore_signal(barrier, 1, device_id={"member": m, "tile": t}, device_id_type=MESH)

    for other in (left, right):
        greet(me, other)
    for r in depth_order:
        greet(*peer(depth, r))
    for r in plane_order:
        greet(*peer(plane, r))

    for copy in loads[2:]:
        copy.wait()
    obs[me] = jnp.broadcast_to(lev_ref[...] * 1024 + col_ref[...], (8, NOBS))
    for copy in loads[:2]:
        copy.wait()

    def turn(x, _):
        q0[x + 2] = state[pl.ds(x, ROWS, stride=X), :]
        wind[x + 1] = courant[pl.ds(x, 2 * LEV, stride=X), :]
        return 0

    for x in (0, 1, 22, 23):
        turn(x, 0)

    pl.semaphore_wait(barrier, 2 + len(plane_order) + len(depth_order))

    halos = [
        remote(q0.at[pl.ds(X, 2)], q0.at[pl.ds(0, 2)], halo_send.at[0], halo_recv.at[0], me, right),
        remote(wind.at[X], wind.at[0], halo_send.at[1], halo_recv.at[1], me, right),
        remote(q0.at[pl.ds(2, 2)], q0.at[pl.ds(X + 2, 2)], halo_send.at[2], halo_recv.at[2], me, left),
        remote(wind.at[1], wind.at[X + 1], halo_send.at[3], halo_recv.at[3], me, left),
    ]
    for copy in halos:
        copy.start()
    obs_copies = []
    for r in (2, 1, 3):
        to = me ^ r
        copy = remote(obs.at[me], obs.at[me], obs_send.at[r - 1], obs_recv.at[r - 1], to, tile)
        copy.start()
        obs_copies.append(copy)

    lax.fori_loop(2, 22, turn, 0, unroll=5)

    def first(i, _):
        q1[i] = upwind(q0[i + 1], q0[i], q0[i + 2], wind[i])
        return 0

    def second(i, _):
        q2[i] = upwind(q1[i + 1], q1[i], q1[i + 2], wind[i + 1])
        return 0

    def pack(i, _):
        field[pl.ds(i, ROWS, stride=X), :] = q2[i]
        return 0

    for i in (2, X - 1):
        first(i, 0)
    lax.fori_loop(3, X - 1, first, 0, unroll=20)
    lax.fori_loop(2, X - 2, second, 0, unroll=20)
    for copy in halos:
        copy.wait_recv()
    for i in (0, 1, X, X + 1):
        first(i, 0)
    for i in (0, 1, X - 2, X - 1):
        second(i, 0)

    outs = [pltpu.make_async_copy(q2, rows_out, out_sem.at[1])]
    outs[0].start()

    for copy in obs_copies:
        copy.wait_recv()

    sub_y = lax.broadcasted_iota(jnp.int32, (CY, NOBS), 0)
    sub_l = lax.broadcasted_iota(jnp.int32, (LEV, NOBS), 0)

    def pick_for(owner):
        code = obs[owner][:1]
        spot = code & 1023
        row = lax.shift_right_logical(code, 10) * 8 + lax.shift_right_logical(spot, 7)
        hot = (sub_y == (spot & 127)).astype(jnp.bfloat16)
        twice = jnp.concatenate([hot, hot], axis=0)
        total = jnp.zeros((LOCAL, LEV, NOBS), jnp.float32)
        for x in range(RUN):
            cells = q2[owner * RUN + x]
            high = cells.astype(jnp.bfloat16)
            rest = cells - high.astype(jnp.float32)
            mid = rest.astype(jnp.bfloat16)
            low = (rest - mid.astype(jnp.float32)).astype(jnp.bfloat16)
            found = jnp.dot(
                jnp.concatenate([high, mid], axis=1), twice, preferred_element_type=jnp.float32
            ) + jnp.dot(low, hot, preferred_element_type=jnp.float32)
            here = (row == sub_l * 8 + x)[None]
            total = total + jnp.where(here, found.reshape(LOCAL, LEV, NOBS), 0.0)
        return jnp.sum(total, axis=1)

    pick_copies = []
    for r in (2, 1, 3):
        to = me ^ r
        pick[r - 1, :LOCAL] = pick_for(to)
        pick[r - 1, LOCAL:] = jnp.zeros((16 - LOCAL, NOBS), jnp.float32)
        copy = remote(pick.at[r - 1], held.at[me], pick_send.at[r - 1], pick_recv.at[r - 1], to, tile)
        copy.start()
        pick_copies.append(copy)
    held[me, :LOCAL] = pick_for(me)
    lax.fori_loop(0, X, pack, 0, unroll=4)
    outs.append(pltpu.make_async_copy(field.at[pl.ds(0, ROWS * X)], field_out, out_sem.at[0]))
    outs[1].start()
    for copy in pick_copies:
        copy.wait_recv()

    picked = jnp.concatenate([held[m][:LOCAL] for m in range(GROUP)], axis=0)
    mean = jnp.sum(picked, axis=0, keepdims=True) * (1.0 / MEMBERS)
    anomaly = (picked - mean) * (1.0 / math.sqrt(MEMBERS - 1.0))
    inverse = 1.0 / var_ref[...]
    scaled = anomaly * inverse
    innov = innov_ref[...] * inverse
    level = lev_ref[...]
    for l in range(LEV):
        at = (l // 3) * 128 + (l % 3) * MEMBERS
        weighted[at : at + MEMBERS] = jnp.where(level == l, scaled, 0.0)
    sub = lax.broadcasted_iota(jnp.int32, (8, NOBS), 0)
    for t in range(6):
        held_here = (level == sub + 3 * t) & (sub < 3)
        weighted[t * 128 + BLOCK : t * 128 + 128] = jnp.where(held_here, innov, 0.0)
    weighted[5 * 128 + MEMBERS : 5 * 128 + BLOCK] = jnp.zeros((BLOCK - MEMBERS, NOBS), jnp.float32)
    sums = lax.dot_general(
        anomaly,
        weighted[...],
        (((1,), (1,)), ((), ())),
        precision=HIGHEST,
        preferred_element_type=jnp.float32,
    )
    for q in range(TILES):
        s, c = q // 6, q % 6
        part[q // piece, (q % piece) * 8 : (q % piece) * 8 + 8] = sums[s * 8 : s * 8 + 8, c * 128 : c * 128 + 128]
    for q in range(TILES, part.shape[0] * piece):
        part[q // piece, (q % piece) * 8 : (q % piece) * 8 + 8] = jnp.zeros((8, 128), jnp.float32)

    def exchange(group, order, source, slots, send, recv):
        for r in order:
            m, t = peer(group, r)
            remote(source(r), slots.at[r - 1], send.at[0], recv.at[0], m, t).start()
        m, t = peer(group, 1)
        whole = remote(slots, slots, send.at[0], recv.at[0], m, t)
        whole.wait_recv()
        return whole

    def tree(values):
        while len(values) > 1:
            values = [values[n] + values[n + 1] for n in range(0, len(values), 2)]
        return values[0]

    sent = [exchange(plane, plane_order, lambda r: part.at[a ^ r], got, rs_send, rs_recv)]
    mine[...] = tree([part[a]] + [got[r] for r in range(len(plane_order))])
    sent.append(exchange(depth, depth_order, lambda r: mine, more, ex_send, ex_recv))
    red[...] = tree([mine[...]] + [more[r] for r in range(len(depth_order))])
    sent.append(exchange(plane, plane_order, lambda r: red, last, ag_send, ag_recv))
    sums_ref[a] = red[...]
    for r in plane_order:
        sums_ref[a ^ r] = last[r - 1]
    outs.append(pltpu.make_async_copy(sums_ref, sums_out.at[pl.ds(0, sums_ref.shape[0])], out_sem.at[2]))
    outs[2].start()

    for copy in halos + obs_copies + pick_copies + sent:
        copy.wait_send()
    for copy in outs:
        copy.wait()


def dot(left, right):
    return jnp.dot(left, right, precision=HIGHEST, preferred_element_type=jnp.float32)


def solve(piece, sums_in, waves_ref, field_ref, coeff_ref, advanced_ref, sums_ref, stack, system, lines, field, wave_at, power_at, sem):
    me = lax.axis_index("member")
    take = pltpu.make_async_copy(sums_in.at[pl.ds(0, sums_ref.shape[0])], sums_ref, sem.at[2])
    take.start()
    fetch = pltpu.make_async_copy(field_ref, field, sem.at[0])
    fetch.start()

    def iota(shape, axis):
        return lax.broadcasted_iota(jnp.int32, shape, axis)

    waves = [waves_ref[j] for j in range(MODES)]
    for j in range(MODES):
        wave_at[j] = 0
        power_at[j] = 0.0
    count = jnp.int32(0)
    for j in range(MODES):
        power = jnp.float32(0.0)
        fresh = jnp.bool_(True)
        for i in range(MODES):
            same = waves[i] == waves[j]
            power = power + jnp.where(same, 1.0 / (1.0 + i), 0.0)
            if i < j:
                fresh = jnp.logical_and(fresh, jnp.logical_not(same))

        @pl.when(fresh)
        def _(count=count, j=j, power=power):
            wave_at[count] = waves[j]
            power_at[count] = power

        count = count + fresh.astype(jnp.int32)

    def cosines(wave, level):
        turn = (wave * (2 * level + 1)) & 63
        turn = jnp.where(turn > 32, 64 - turn, turn)
        back = turn > 16
        turn = jnp.where(back, 32 - turn, turn)
        angle = turn.astype(jnp.float32) * (math.pi / 32.0)
        square = angle * angle
        value = jnp.full(square.shape, 1.0 / math.factorial(14), jnp.float32)
        for n in (12, 10, 8, 6, 4, 2, 0):
            value = 1.0 / math.factorial(n) - value * square
        return jnp.where(back, -value, value)

    level = iota((LEV, 128), 0)
    lane = iota((LEV, 128), 1)
    columns = []
    for i in range(MODES):
        wave = jnp.full((LEV, 128), wave_at[i], jnp.int32)
        columns.append(jnp.sqrt(jnp.full((LEV, 128), power_at[i], jnp.float32)) * cosines(wave, level))
    across = []
    for c in range(4):
        value = jnp.where(lane < 40, columns[3 * c], jnp.where(lane < 80, columns[3 * c + 1], columns[3 * c + 2]))
        across.append(jnp.where(lane < BLOCK, value, 1.0 if c == 3 else 0.0))

    segment = iota((MEMBERS, 128), 1)
    seg0 = segment < 40
    seg1 = segment < 80
    seg2 = segment < BLOCK
    take.wait()
    for t in range(6):
        tile = jnp.concatenate(
            [
                sums_ref[(s * 6 + t) // piece, ((s * 6 + t) % piece) * 8 : ((s * 6 + t) % piece) * 8 + 8]
                for s in range(5)
            ],
            axis=0,
        )
        shifts = {0: tile}
        for d in (1, 2, -1, -2) if t < 5 else (1, 2):
            shifts[d] = pltpu.roll(tile, (40 * d) % 128, 1)
        for u in range(3 if t < 5 else 1):
            last = tile if u == 0 else pltpu.roll(tile, 128 - u, 1)
            stack[3 * t + u] = jnp.where(
                seg0, shifts[-u], jnp.where(seg1, shifts[1 - u], jnp.where(seg2, shifts[2 - u], last))
            )

    row = iota((MEMBERS, 128), 0)
    for i in range(MODES):

        @pl.when(i < count)
        def _(i=i):
            totals = [jnp.zeros((MEMBERS, 128), jnp.float32) for _ in range(4)]
            for c in range(4):
                if c == i // 3:
                    totals[c] = jnp.where(segment == row + 40 * (i % 3), 1.0, 0.0)
            factors = [columns[i] * across[c] for c in range(4)]
            for l in range(LEV):
                gram = stack[l]
                for c in range(4):
                    totals[c] = totals[c] + gram * factors[c][l : l + 1]
            for c in range(4):
                system[i * MEMBERS : (i + 1) * MEMBERS, c * 128 : (c + 1) * 128] = totals[c]

    fetch.wait()
    keep = pltpu.make_async_copy(field, advanced_ref, sem.at[1])
    keep.start()
    lines[...] = jnp.zeros(lines.shape, jnp.float32)
    wide = (8, 128)
    sub = iota(wide, 0)

    def spread(x):
        return jnp.broadcast_to(x, wide)

    def clear(s, rows_at, first):
        if rows_at.stop <= rows_at.start:
            return
        c0 = s // 3
        cols = slice(first * 128, 512)
        system[rows_at, cols] = system[rows_at, cols] - dot(
            system[rows_at, c0 * 128 : (c0 + 1) * 128], lines[s % 2, :, cols]
        )

    def deferred(s, first):
        edges = [(s + 1) * MEMBERS + AHEAD, (s + 2) * MEMBERS, (s + 3) * MEMBERS, MODES * MEMBERS]
        for start, stop in zip(edges[:-1], edges[1:]):
            clear(s, slice(start, min(stop, MODES * MEMBERS)), first)
        clear(s, slice(0, s * MEMBERS), first)

    def eliminate(s):
        c0, offset = s // 3, (s % 3) * MEMBERS
        tiles = list(range(c0, 4))
        base = s * MEMBERS
        extra = list(range(5, 5 + AHEAD // 8)) if s + 1 < MODES else []

        def spot(t, c):
            return slice(base + 8 * t, base + 8 * t + 8), slice(c * 128, (c + 1) * 128)

        if s >= 2:
            before = ((s - 2) % 3) * MEMBERS
            lines[s % 2, before : before + MEMBERS] = jnp.zeros((MEMBERS, 512), jnp.float32)
        if s > 0:
            deferred(s - 1, c0)
        for p in range(5):
            at = [offset + 8 * p + j for j in range(8)]
            pivot = [system[spot(p, c)] for c in tiles]
            cols = [spread(pivot[0][:, n : n + 1]) for n in at]
            keep_row = swap_row = jnp.zeros(wide, jnp.float32)
            for j in range(0, 8, 2):
                c1, c2 = cols[j], cols[j + 1]
                a, b = spread(c1[j : j + 1]), spread(c2[j : j + 1])
                b2, d = spread(c1[j + 1 : j + 2]), spread(c2[j + 1 : j + 2])
                inv = 1.0 / (a * d - b * b2)
                s1, s2 = sub == j, sub == j + 1
                m1 = jnp.where(s1 | s2, 0.0, c1 * d - c2 * b2) * inv
                m2 = jnp.where(s1 | s2, 0.0, c2 * a - c1 * b) * inv
                keep_row = jnp.where(s1, d * inv, jnp.where(s2, a * inv, keep_row))
                swap_row = jnp.where(s1, b * inv, jnp.where(s2, b2 * inv, swap_row))

                def step(v):
                    return v - (m1 * spread(v[j : j + 1]) + m2 * spread(v[j + 1 : j + 2]))

                cols[j + 2 :] = [step(v) for v in cols[j + 2 :]]
                pivot = [step(v) for v in pivot]
            line = {}
            for n, c in enumerate(tiles):
                v = pivot[n]
                swapped = jnp.where(sub % 2 == 0, pltpu.roll(v, 7, 0), pltpu.roll(v, 1, 0))
                v = keep_row * v - swap_row * swapped
                system[spot(p, c)] = v
                for j in range(8):
                    line[c, j] = spread(v[j : j + 1])
            for t in [(p + d) % 5 for d in range(1, 5)] + extra:
                head = system[spot(t, c0)]
                multipliers = [spread(head[:, n : n + 1]) for n in at]
                for c in tiles:
                    prods = [multipliers[j] * line[c, j] for j in range(8)]
                    while len(prods) > 1:
                        prods = [prods[k] + prods[k + 1] for k in range(0, len(prods), 2)]
                    system[spot(t, c)] = system[spot(t, c)] - prods[0]
        for t in range(5):
            for c in tiles:
                lines[s % 2, offset + 8 * t : offset + 8 * t + 8, c * 128 : (c + 1) * 128] = system[spot(t, c)]

    for s in range(MODES):

        @pl.when(s < count)
        def _(s=s):
            eliminate(s)

    for s in range(1, MODES):

        @pl.when(s + 1 == count)
        def _(s=s):
            clear(s, slice(0, s * MEMBERS), 3)

    for i in range(MODES):
        weight = jnp.broadcast_to(
            system[i * MEMBERS : (i + 1) * MEMBERS, 384:512][:, BLOCK : BLOCK + 1], (MEMBERS, 128)
        )
        weight = (weight - jnp.sum(weight, axis=0, keepdims=True) * (1.0 / MEMBERS)) * (
            1.0 / math.sqrt(MEMBERS - 1.0)
        )
        stack[i, :MEMBERS] = weight
    for i in range(MODES):

        @pl.when(i >= count)
        def _(i=i):
            stack[i, :MEMBERS] = jnp.zeros((MEMBERS, 128), jnp.float32)

    for k in range(LOCAL):
        total = jnp.zeros((LEV, 128), jnp.float32)
        for i in range(MODES):
            total = total + columns[i] * stack[i, pl.ds(me * LOCAL + k, 1)]
        coeff_ref[k] = total
    keep.wait()


def finish(coeff_in, rows_ref, out_ref, coeff_ref, rows, part, got, load_sem, send_sem, recv_sem):
    me = lax.axis_index("member")
    tile = lax.axis_index("tile")
    barrier = pltpu.get_barrier_semaphore()
    for r in (2, 1, 3):
        pl.semaphore_signal(barrier, 1, device_id={"member": me ^ r, "tile": tile}, device_id_type=MESH)
    loads = [
        pltpu.make_async_copy(rows_ref, rows, load_sem.at[0]),
        pltpu.make_async_copy(coeff_in, coeff_ref, load_sem.at[1]),
    ]
    for copy in loads:
        copy.start()

    def run_for(owner, slot):
        for x in range(RUN):
            total = jnp.zeros((LEV, CY), jnp.float32)
            for k in range(LOCAL):
                total = total + rows[owner * RUN + x, k * LEV : (k + 1) * LEV] * coeff_ref[k]
            part[slot, x] = total

    for copy in loads:
        copy.wait()
    copies = []
    for r in (2, 1, 3):
        to = me ^ r
        run_for(to, r)
        if not copies:
            pl.semaphore_wait(barrier, GROUP - 1)
        copy = remote(part.at[r], got.at[r - 1], send_sem.at[r - 1], recv_sem.at[r - 1], to, tile)
        copy.start()
        copies.append(copy)
    run_for(me, 0)
    for copy in copies:
        copy.wait_recv()
    for x in range(RUN):
        out_ref[:, x * CY : (x + 1) * CY] = (part[0, x] + got[0, x]) + (got[1, x] + got[2, x])
    for copy in copies:
        copy.wait_send()


def on_device(member_state, courant, obs_col, obs_lev, innovation, obs_var, mode_waves):
    tiles = lax.axis_size("tile")
    n_z = tiles // (N_Y * N_CORE)
    plane = ((2, None), (N_Y.bit_length() - 1, 1))
    depth = ((n_z.bit_length() - 1, N_Y.bit_length()), (1, 0))
    g1 = GROUP * N_Y
    g2 = n_z * N_CORE
    piece = -(-TILES // g1)
    f32 = jnp.float32
    dma = pltpu.SemaphoreType.DMA
    shape = member_state.shape
    field, rows, sums = pl.pallas_call(
        functools.partial(front, plane, depth, piece),
        out_shape=[
            jax.ShapeDtypeStruct((ROWS * X, CY), f32),
            jax.ShapeDtypeStruct((X, ROWS, CY), f32),
            jax.ShapeDtypeStruct((16 * g1, piece * 8, 128), f32),
        ],
        in_specs=[ANY] * 6,
        out_specs=[ANY, ANY, ANY],
        scratch_shapes=[
            pltpu.VMEM((ROWS * X + X, CY), f32),
            pltpu.VMEM((2 * LEV * X + X, CY), f32),
            pltpu.VMEM((X + 4, ROWS, CY), f32),
            pltpu.VMEM((X + 2, ROWS, CY), f32),
            pltpu.VMEM((X, ROWS, CY), f32),
            pltpu.VMEM((X + 2, 2 * LEV, CY), f32),
            pltpu.VMEM((ROWS * X + X, CY), f32),
            pltpu.VMEM((1, NOBS), jnp.int32),
            pltpu.VMEM((1, NOBS), jnp.int32),
            pltpu.VMEM((1, NOBS), f32),
            pltpu.VMEM((1, NOBS), f32),
            pltpu.VMEM((GROUP, 8, NOBS), jnp.int32),
            pltpu.VMEM((GROUP - 1, 16, NOBS), f32),
            pltpu.VMEM((GROUP, 16, NOBS), f32),
            pltpu.VMEM((WIDE, NOBS), f32),
            pltpu.VMEM((g1, piece * 8, 128), f32),
            pltpu.VMEM((g1 - 1, piece * 8, 128), f32),
            pltpu.VMEM((piece * 8, 128), f32),
            pltpu.VMEM((piece * 8, 128), f32),
            pltpu.VMEM((g2 - 1, piece * 8, 128), f32),
            pltpu.VMEM((g1 - 1, piece * 8, 128), f32),
            pltpu.VMEM((g1, piece * 8, 128), f32),
            dma((6,)),
            dma((4,)),
            dma((4,)),
            dma((GROUP - 1,)),
            dma((GROUP - 1,)),
            dma((GROUP - 1,)),
            dma((GROUP - 1,)),
            dma((1,)),
            dma((1,)),
            dma((1,)),
            dma((1,)),
            dma((1,)),
            dma((1,)),
            dma((3,)),
        ],
        compiler_params=pltpu.CompilerParams(
            collective_id=0, has_side_effects=True, vmem_limit_bytes=FRONT_VMEM
        ),
        name="front",
    )(
        member_state.reshape(ROWS * X, CY),
        courant.reshape(2 * LEV * X, CY),
        obs_col.reshape(1, NOBS),
        obs_lev.reshape(1, NOBS),
        innovation.reshape(1, NOBS),
        obs_var.reshape(1, NOBS),
    )
    coeffs, advanced = pl.pallas_call(
        functools.partial(solve, piece),
        out_shape=[
            jax.ShapeDtypeStruct((LOCAL, LEV, CY), f32),
            jax.ShapeDtypeStruct((ROWS * X, CY), f32),
        ],
        in_specs=[ANY, SMEM, ANY],
        out_specs=[VMEM, ANY],
        scratch_shapes=[
            pltpu.VMEM((g1, piece * 8, 128), f32),
            pltpu.VMEM((LEV, MEMBERS, 128), f32),
            pltpu.VMEM((MODES * MEMBERS, 512), f32),
            pltpu.VMEM((2, 128, 512), f32),
            pltpu.VMEM((ROWS * X, CY), f32),
            pltpu.SMEM((MODES,), jnp.int32),
            pltpu.SMEM((MODES,), f32),
            dma((3,)),
        ],
        compiler_params=pltpu.CompilerParams(vmem_limit_bytes=SOLVE_VMEM),
        name="solve",
    )(sums, mode_waves, field)
    increment = pl.pallas_call(
        finish,
        out_shape=jax.ShapeDtypeStruct((LEV, RUN * CY), f32),
        in_specs=[ANY, ANY],
        out_specs=VMEM,
        scratch_shapes=[
            pltpu.VMEM((LOCAL, LEV, CY), f32),
            pltpu.VMEM((X, ROWS, CY), f32),
            pltpu.VMEM((GROUP, RUN, LEV, CY), f32),
            pltpu.VMEM((GROUP - 1, RUN, LEV, CY), f32),
            dma((2,)),
            dma((GROUP - 1,)),
            dma((GROUP - 1,)),
        ],
        compiler_params=pltpu.CompilerParams(
            collective_id=1, has_side_effects=True, vmem_limit_bytes=FINISH_VMEM
        ),
        name="finish",
    )(coeffs, rows)
    return advanced.reshape(shape), increment


def solution(mesh):
    in_specs = (
        P("member", None, "tile", None),
        P(None, None, "tile", None),
        P(("member", "tile")),
        P(("member", "tile")),
        P(("member", "tile")),
        P(("member", "tile")),
        P(),
    )
    out_specs = (P("member", None, "tile", None), P(None, ("member", "tile")))
    return jax.shard_map(
        on_device, mesh=mesh, in_specs=in_specs, out_specs=out_specs, check_vma=False
    )
```
